128 devices in a mesh: seq: 32 (over x, z, core), head: 4 (over y).
Axes of the slice: x: 4, y: 4, z: 4, core: 2. Of those that a mesh axis runs over, the one named last changes fastest.
Arguments:
- tokens: bfloat16 [12288, 2240], P('seq'), may hold values from -40 to 40
- w_query: bfloat16 [2240, 2240], P(None, 'head'), may hold values from -0.125 to 0.125
- w_key: bfloat16 [2240, 2240], P(None, 'head'), may hold values from -0.125 to 0.125
- w_value: bfloat16 [2240, 2240], P(None, 'head'), may hold values from -0.125 to 0.125
- w_out: bfloat16 [2240, 2240], P('head'), may hold values from -0.125 to 0.125
- grad_out: bfloat16 [12288, 2240], P('seq'), may hold values from -6 to 6
Outputs:
- attn_out: bfloat16 [12288, 2240], P('seq', 'head')
- grad_tokens: bfloat16 [12288, 2240], P('seq', 'head')
- grad_query: float32 [2240, 2240], P('seq', 'head')
- grad_key: float32 [2240, 2240], P('seq', 'head')
- grad_value: float32 [2240, 2240], P('seq', 'head')
- grad_wout: float32 [2240, 2240], P('head', 'seq')
The draws below stay inside these ranges and needn't reach their ends.
All inputs are finite; a program needn't handle non-finite values.
Results may differ from the reference program's by a relative error of at most 0.018.
Values sent between devices are 32-bit elements; how exact they have to be, the bound alone decides.
A program may use at most 128 MiB of HBM per device.

```python
import math
import jax
import jax.numpy as jnp
from jax import lax

D = 2240
HEADS = 20
HEAD_DIM = 112
TOK_DEV = 384
TOKENS = 12288


def draw_tokens(key, part):
    key = jax.random.fold_in(key, 11)
    key_noise, key_scale = jax.random.split(key, 2)
    blocks = TOKENS // TOK_DEV
    width = D // blocks
    ramp = 0.6 + 0.6 * jnp.arange(blocks, dtype=jnp.float32) / max(blocks - 1, 1)
    owner = jnp.arange(D) // width
    boost = jnp.where(owner[None, :] == jnp.arange(blocks)[:, None], 3.0, 1.0) * ramp[:, None]
    column_scale = jnp.repeat(boost, TOK_DEV, axis=0)
    noise = jnp.clip(jax.random.normal(key_noise, (TOKENS, D), jnp.float32), -5.0, 5.0)
    row_scale = jnp.exp(jax.random.uniform(key_scale, (TOKENS,), jnp.float32, jnp.log(0.5), jnp.log(2.0)))
    return jnp.clip(noise * row_scale[:, None] * column_scale, -40.0, 40.0).astype(jnp.bfloat16)


def strengthened(array, own_key, source, target, shards_of, factor):
    def block_of(axis_at):
        return (jnp.arange(array.shape[axis_at]) // (array.shape[axis_at] // shards_of)).reshape((-1,) + (1,) * (array.ndim - 1 - axis_at))

    first = jax.random.permutation(own_key, shards_of)[block_of(target)]
    far = (block_of(target) + shards_of // 2) % shards_of
    return jnp.where((block_of(source) == first) | (block_of(source) == far), factor * array, array)


def block_scale(key, shape, cuts, low, high):
    def one(position, blocks):
        steps = jax.random.uniform(jax.random.fold_in(jax.random.fold_in(key, 6), position), (blocks,), jnp.float32, low / len(cuts), high / len(cuts))
        return jnp.repeat(jnp.exp(steps), shape[position] // blocks).reshape((-1,) + (1,) * (len(shape) - position - 1))

    factor_of = one(*cuts[0])
    for cut in cuts[1:]:
        factor_of = factor_of * one(*cut)
    return factor_of


def bell_draw(own_key, shape, spread, most, cuts=(), held_as=jnp.bfloat16):
    level = block_scale(own_key, shape, cuts, -0.22, 0.18) if cuts else 1.0
    values = jax.random.normal(own_key, shape, jnp.float32) * spread * level
    return jnp.minimum(jnp.maximum(values, -most), most).astype(held_as)


def heavy_noise(key, shape, deviation, limit, pieces, heavy, kind=jnp.bfloat16):
    entries = deviation * jax.random.normal(key, shape, jnp.float32)
    if pieces:
        entries = entries * block_scale(key, shape, pieces, -0.22, 0.18)
    return jnp.clip(strengthened(entries, jax.random.fold_in(key, 3), *heavy), -limit, limit).astype(kind)


def setup_inputs(seed: int = 0) -> dict:
    seeds = jax.random.split(jax.random.key(seed), 7)
    return {
        "tokens": draw_tokens(jax.random.fold_in(seeds[6], 71), 0),
        "w_query": bell_draw(seeds[1], (D, D), D ** -0.5, 0.125, ((1, 4),)),
        "w_key": bell_draw(seeds[2], (D, D), D ** -0.5, 0.125, ((1, 4),)),
        "w_value": bell_draw(seeds[3], (D, D), D ** -0.5, 0.125, ((1, 4),)),
        "w_out": bell_draw(seeds[4], (D, D), D ** -0.5, 0.125, ((0, 4),)),
        "grad_out": heavy_noise(seeds[5], (TOKENS, D), 1.0, 6.0, ((0, 32),), (0, 1, 32, 2.75)),
    }


epsilon = 1e-15
exact = lax.Precision.HIGHEST

def reference(tokens, w_query, w_key, w_value, w_out, grad_out):
    total_rows = tokens.shape[0]
    f32 = jnp.float32
    queries = jax.nn.relu(jnp.dot(tokens, w_query, preferred_element_type=f32)).astype(jnp.bfloat16)
    key_feat = jax.nn.relu(jnp.dot(tokens, w_key, preferred_element_type=f32)).astype(jnp.bfloat16)
    val_feat = jnp.dot(tokens, w_value, preferred_element_type=f32).astype(jnp.bfloat16)
    query_heads = queries.astype(f32).reshape(total_rows, HEADS, HEAD_DIM)
    key_heads = key_feat.astype(f32).reshape(total_rows, HEADS, HEAD_DIM)
    value_heads = val_feat.astype(f32).reshape(total_rows, HEADS, HEAD_DIM)
    kv_state = jnp.einsum('thc,the->hce', key_heads, value_heads, precision=exact)
    key_sum = lax.optimization_barrier(jnp.sum(key_heads, axis=0))
    numerator = jnp.einsum('thc,hce->the', query_heads, kv_state, precision=exact)
    denominator = jnp.einsum('thc,hc->th', query_heads, key_sum, precision=exact) + epsilon
    attended = numerator / denominator[..., None]
    mixed = attended.reshape(total_rows, D).astype(jnp.bfloat16)
    attn_out = jnp.dot(mixed, w_out, preferred_element_type=f32).astype(jnp.bfloat16)
    grad_mixed = jnp.dot(grad_out, w_out.T, preferred_element_type=f32).astype(jnp.bfloat16)
    upstream = grad_mixed.astype(f32).reshape(total_rows, HEADS, HEAD_DIM)
    num_grad = upstream / denominator[..., None]
    den_grad = -lax.optimization_barrier(jnp.sum(upstream * attended, axis=-1)) / denominator
    grad_state = jnp.einsum('thc,the->hce', query_heads, num_grad, precision=exact)
    grad_ksum = jnp.einsum('th,thc->hc', den_grad, query_heads, precision=exact)
    dq_full = jnp.einsum('the,hce->thc', num_grad, kv_state, precision=exact) + den_grad[..., None] * key_sum[None]
    dk_full = jnp.einsum('the,hce->thc', value_heads, grad_state, precision=exact) + grad_ksum[None]
    dv_full = jnp.einsum('thc,hce->the', key_heads, grad_state, precision=exact)
    dq_pre = jnp.where(query_heads > 0, dq_full, 0.0).reshape(total_rows, D).astype(jnp.bfloat16)
    dk_pre = jnp.where(key_heads > 0, dk_full, 0.0).reshape(total_rows, D).astype(jnp.bfloat16)
    dv_pre = dv_full.reshape(total_rows, D).astype(jnp.bfloat16)
    grad_tokens = (jnp.dot(dq_pre, w_query.T, preferred_element_type=f32) + jnp.dot(dk_pre, w_key.T, preferred_element_type=f32) + jnp.dot(dv_pre, w_value.T, preferred_element_type=f32)).astype(jnp.bfloat16)
    factor = 1.0 / math.sqrt(TOKENS)
    grad_query = jnp.dot(tokens.T, dq_pre, preferred_element_type=f32) * factor
    grad_key = jnp.dot(tokens.T, dk_pre, preferred_element_type=f32) * factor
    grad_value = jnp.dot(tokens.T, dv_pre, preferred_element_type=f32) * factor
    grad_wout = jnp.dot(mixed.T, grad_out, preferred_element_type=f32) * factor
    return (attn_out, grad_tokens, grad_query, grad_key, grad_value, grad_wout)
```

```python
import functools
import math

import jax
import jax.numpy as jnp
from jax import lax
from jax.experimental import pallas as pl
from jax.experimental.pallas import tpu as pltpu
from jax.sharding import PartitionSpec as P

f32 = jnp.float32
bf16 = jnp.bfloat16
MESH = pl.DeviceIdType.MESH

D = 2240
W = 560
WP = 640
T = 384
HD = 112
ROWS = 70
RP = 72
NB = 16
GR = NB * RP
GC = 1152
CH = 4 * RP
SR = 576
EPS = 1e-15


def dot(a, b):
    return lax.dot_general(a, b, (((1,), (0,)), ((), ())), preferred_element_type=f32)


def dot_t(a, b):
    return lax.dot_general(a, b, (((1,), (1,)), ((), ())), preferred_element_type=f32)


def dot_n(a, b):
    return lax.dot_general(a, b, (((0,), (0,)), ((), ())), preferred_element_type=f32)


def parts(v):
    high = v.astype(bf16)
    return high, (v - high.astype(f32)).astype(bf16)


def head_of(index):
    total = jnp.zeros_like(index)
    for edge in (112, 224, 336, 448, 560):
        total = total + (index >= edge).astype(jnp.int32)
    return total


def same_head(row0, rows, col0, cols):
    r = lax.broadcasted_iota(jnp.int32, (rows, cols), 0) + row0
    c = lax.broadcasted_iota(jnp.int32, (rows, cols), 1) + col0
    return head_of(r) == head_of(c)


def loop(count, fn):
    def step(i, carry):
        fn(i)
        return carry

    lax.fori_loop(0, count, step, 0)


class Copies:
    def __init__(self, send, recv):
        self.send, self.recv, self.used, self.open = send, recv, 0, []

    def start(self, src, dst, device):
        k = self.used
        self.used += 1
        copy = pltpu.make_async_remote_copy(
            src_ref=src, dst_ref=dst, send_sem=self.send.at[k], recv_sem=self.recv.at[k],
            device_id=device, device_id_type=MESH)
        copy.start()
        self.open.append(copy)
        return copy

    def sent(self, copy):
        copy.wait_send()
        self.open = [other for other in self.open if other is not copy]

    def finish(self):
        for copy in self.open:
            copy.wait_send()
        self.open = []


class Ring:
    def __init__(self, copies, left, right, slot, box, cut):
        self.copies, self.left, self.right, self.slot = copies, left, right, slot
        self.box, self.cut = box, cut
        self.rows = box.shape[1]

    def land(self, kind, half):
        if half == 0:
            return self.box.at[kind, pl.ds(0, self.cut), :]
        return self.box.at[kind, pl.ds(self.cut, self.rows - self.cut), :]

    def far(self):
        self.a0 = self.copies.start(self.slot("far", 0), self.land(0, 0), self.right)
        self.a1 = self.copies.start(self.slot("far", 1), self.land(0, 1), self.left)

    def near_right(self):
        self.d1 = self.copies.start(self.slot("right", 1), self.land(1, 1), self.right)

    def near_left(self):
        self.d0 = self.copies.start(self.slot("left", 0), self.land(1, 0), self.left)

    def combine(self):
        self.a0.wait_recv()
        ref = self.slot("right", 0)
        ref[...] = ref[...] + self.land(0, 0)[...]
        self.c0 = self.copies.start(ref, self.land(2, 0), self.right)
        self.a1.wait_recv()
        ref = self.slot("left", 1)
        ref[...] = ref[...] + self.land(0, 1)[...]
        self.c1 = self.copies.start(ref, self.land(2, 1), self.left)

    def arrived(self):
        for copy in (self.d0, self.d1, self.c0, self.c1):
            copy.wait_recv()

    def sent(self, names):
        for name in names:
            self.copies.sent(getattr(self, name))


def kernel(tok_h, wq_h, wk_h, wv_h, wo_h, go_h,
           at_o, gt_o, g1_o, g2_o,
           tok, go, wslot, wo, wot, tokt, got,
           q, k, v, gm, mx, ngh, ngl, dg, kvh, kvl, ones,
           send, recv, rhs, gbuf, own1, own2, box1, box2, pbox1, pbox2,
           cp, dp, cbox, dbox,
           sta, a0, a1, a2, afin, asum, stb, b0, b1, b2, bfin, bsum,
           in_sem, w_sem, out_sem, ssem, rsem):
    s = lax.axis_index("seq")
    y = lax.axis_index("head")
    c = s % 2
    chip = s // 2
    x = chip // 4
    z = chip % 4
    fa = x * (1 - c) + z * c
    sa = z * (1 - c) + x * c

    def first(i):
        return {"seq": ((i * (1 - c) + sa * c) * 4 + sa * (1 - c) + i * c) * 2 + c, "head": y}

    def second(i):
        return {"seq": ((fa * (1 - c) + i * c) * 4 + i * (1 - c) + fa * c) * 2 + c, "head": y}

    def along_y(i):
        return {"seq": s, "head": i}

    partner = {"seq": s + 1 - 2 * c, "head": y}

    def local(src, dst, sem):
        copy = pltpu.make_async_copy(src, dst, sem)
        copy.start()
        return copy

    in_tok = local(tok_h, tok, in_sem.at[0])
    in_k = local(wk_h, wslot.at[0], in_sem.at[1])
    in_v = local(wv_h, wslot.at[1], in_sem.at[2])
    in_go = local(go_h, go, in_sem.at[3])
    in_wo = local(wo_h, wo, in_sem.at[4])

    barrier = pltpu.get_barrier_semaphore()
    peers = [partner, along_y((y + 1) % 4), along_y((y + 3) % 4)]
    peers += [first((fa + d) % 4) for d in (1, 2, 3)]
    peers += [second((sa + d) % 4) for d in (1, 2, 3)]
    for peer in peers:
        pl.semaphore_signal(barrier, inc=1, device_id=peer, device_id_type=MESH)

    copies = Copies(ssem, rsem)

    for ref in (q, k, v, gm):
        ref[:, 512:WP] = jnp.zeros((T, WP - 512), bf16)

    def project(src, weight, dst, act):
        def tile(i):
            r = pl.ds(pl.multiple_of(i * 128, 128), 128)
            value = dot(src[r, :], weight[...])
            if act:
                value = jnp.maximum(value, 0.0)
            dst[r, 0:W] = value.astype(bf16)

        loop(T // 128, tile)

    def pack_state(st, left, rights, sums):
        for i in range(5):
            total = None
            for right in rights:
                block = dot_n(left[:, 128 * i:128 * i + 128], right[...])
                total = block if total is None else total + block
            total = jnp.where(same_head(128 * i, 128, 0, WP), total, 0.0)
            folded = total[:, 0:128]
            for j in range(1, 5):
                folded = folded + total[:, 128 * j:128 * j + 128]
            height = min(128, SR - 128 * i)
            st[128 * i:128 * i + height, :] = folded[:height, :]
        for j in range(5):
            st[W + j:W + j + 1, :] = sums[:, 128 * j:128 * j + 128]

    def unpack_state(fin):
        def tile(r0, rows, keep):
            block = fin[r0:r0 + rows, :]
            if keep < rows:
                block = jnp.where(lax.broadcasted_iota(jnp.int32, (rows, 128), 0) < keep, block, 0.0)
            for j in range(5):
                high, low = parts(jnp.where(same_head(r0, rows, 128 * j, 128), block, 0.0))
                kvh[r0:r0 + rows, 128 * j:128 * j + 128] = high
                kvl[r0:r0 + rows, 128 * j:128 * j + 128] = low

        for i in range(4):
            tile(128 * i, 128, 128)
        tile(512, 64, 48)

    def sums_row(fin):
        return jnp.concatenate([fin[W + j:W + j + 1, :] for j in range(5)], axis=1)

    half = SR // 2
    piece = half // 4
    mine = pl.multiple_of(c * half, 8)
    other = pl.multiple_of((1 - c) * half, 8)

    def mine_piece(i):
        return pl.ds(pl.multiple_of(c * half + i * piece, 8), piece)

    class State:
        def __init__(self, st, r0, r1, r2, fin, total):
            self.st, self.r0, self.r1, self.r2, self.fin, self.total = st, r0, r1, r2, fin, total

        def step0(self):
            self.c = copies.start(self.st.at[pl.ds(other, half), :], self.r0, partner)

        def step1(self):
            self.c.wait_recv()
            rows = pl.ds(mine, half)
            self.st[rows, :] = self.st[rows, :] + self.r0[...]
            self.cs = [copies.start(self.st.at[mine_piece((fa + d) % 4), :], self.r1.at[d - 1],
                                    first((fa + d) % 4)) for d in (1, 2, 3)]

        def step2(self):
            for copy in self.cs:
                copy.wait_recv()
            self.total[...] = (self.st[mine_piece(fa), :] + self.r1[0]) + (self.r1[1] + self.r1[2])
            self.cs = [copies.start(self.total, self.r2.at[d - 1], second((sa + d) % 4))
                       for d in (1, 2, 3)]

        def step3(self):
            for copy in self.cs:
                copy.wait_recv()
            rows = mine_piece(fa)
            self.fin[rows, :] = (self.total[...] + self.r2[0]) + (self.r2[1] + self.r2[2])
            self.cs = [copies.start(self.fin.at[rows, :], self.fin.at[rows, :], first((fa + d) % 4))
                       for d in (1, 2, 3)]

        def step4(self):
            for copy in self.cs:
                copy.wait_recv()
            rows = pl.ds(mine, half)
            self.c = copies.start(self.fin.at[rows, :], self.fin.at[rows, :], partner)

        def done(self):
            self.c.wait_recv()

    in_tok.wait()
    in_k.wait()
    project(tok, wslot.at[0], k, True)
    in_q = local(wq_h, wslot.at[0], in_sem.at[5])
    in_v.wait()
    project(tok, wslot.at[1], v, False)
    pack_state(sta, k, [v], jnp.sum(k[...].astype(f32), axis=0, keepdims=True))
    pl.semaphore_wait(barrier, len(peers))
    state = State(sta, a0, a1, a2, afin, asum)
    state.step0()

    in_q.wait()
    project(tok, wslot.at[0], q, True)
    state.step1()

    ring_y = {"far": (y + 2) % 4, "right": (y + 1) % 4, "left": (y + 3) % 4, "own": y}

    def fetch(which, place):
        rows = pl.ds(pl.multiple_of(ring_y[which] * W, 16), W)
        return [local(w.at[rows, :], wslot.at[place, pl.ds(W * i, W), :], w_sem.at[place, i])
                for i, w in enumerate((wq_h, wk_h, wv_h))]

    fetch_far = fetch("far", 0)
    fetch_right = fetch("right", 1)

    def gather_rows(src, base, which):
        for b in range(NB):
            lo = 2 * ROWS * b
            w0 = lo // 128 * 128
            w1 = min(D, -(-(lo + 2 * ROWS) // 128) * 128)
            i = lax.broadcasted_iota(jnp.int32, (RP, w1 - w0), 0)
            j = lax.broadcasted_iota(jnp.int32, (RP, w1 - w0), 1)
            pick = jnp.logical_and(j == i + (lo - w0) + ROWS * which, i < ROWS)
            value = dot_t(pick.astype(f32).astype(bf16), src[:, w0:w1])
            place = b * (1 - which) + (b % 4 * 4 + b // 4) * which
            cp[pl.ds(pl.multiple_of(base + place * RP, 8), RP), :] = value

    def rows_of(src, dst, base):
        gather_rows(src, base, c)

        def cast(i):
            r = pl.multiple_of(i * 288, 16)
            dst[pl.ds(r, 288), 0:T] = cp[pl.ds(pl.multiple_of(base + r, 8), 288), :].astype(bf16)

        loop(GR // 288, cast)
        gather_rows(src, base, 1 - c)
        place = pl.ds(base, GR)
        return copies.start(cp.at[place, :], dp.at[place, :], partner)

    send_tok = rows_of(tok, tokt, 0)
    state.step2()

    in_wo.wait()
    in_go.wait()

    def mixed_grad(i):
        r = pl.ds(pl.multiple_of(i * 128, 128), 128)
        gm[r, 0:W] = dot_t(go[r, :], wo[...]).astype(bf16)

    loop(T // 128, mixed_grad)
    state.step3()
    send_go = rows_of(go, got, GR)
    state.step4()

    for j in range(0, D, 256):
        n = min(256, D - j)
        eye = (lax.broadcasted_iota(jnp.int32, (n, n), 0) == lax.broadcasted_iota(jnp.int32, (n, n), 1))
        wot[j:j + n, :] = dot_t(eye.astype(f32).astype(bf16), wo[:, j:j + n]).astype(bf16)
    for i in range(5):
        ones[128 * i:128 * i + 128, :] = same_head(128 * i, 128, 0, WP).astype(f32).astype(bf16)
    kvh[SR:WP, :] = jnp.zeros((WP - SR, WP), bf16)
    kvl[SR:WP, :] = jnp.zeros((WP - SR, WP), bf16)

    state.done()
    unpack_state(afin)
    ksum = sums_row(afin)

    def attend(i):
        r = pl.ds(pl.multiple_of(i * 128, 128), 128)
        qt = q[r, :]
        num = dot(qt, kvh[...]) + dot(qt, kvl[...])
        high, low = parts(qt.astype(f32) * ksum)
        rec = 1.0 / (dot(high, ones[...]) + dot(low, ones[...]) + EPS)
        att = num * rec
        mx[r, :] = att.astype(bf16)
        g = gm[r, :].astype(f32)
        high, low = parts(g * rec)
        ngh[r, :] = high
        ngl[r, :] = low
        high, low = parts(g * att)
        dg[r, :] = -(dot(high, ones[...]) + dot(low, ones[...])) * rec

    loop(T // 128, attend)

    send_tok.wait_recv()
    copies.sent(send_tok)
    send_go.wait_recv()
    copies.sent(send_go)
    order = {"far": 0, "right": 1, "left": 2, "own": 3}

    def out_chunk(which):
        rows = pl.ds(pl.multiple_of(ring_y[which] * W, 16), W)
        cp[pl.ds(order[which] * W, W), :] = dot_t(wot[rows, :], mx[:, 0:W])

    def y_slot(buf):
        def slot(which, h):
            return buf.at[pl.ds(order[which] * W + h * (W // 2), W // 2), :]

        return slot

    up, down = along_y((y + 1) % 4), along_y((y + 3) % 4)
    ring_c = Ring(copies, down, up, y_slot(cp), cbox, W // 2)
    out_chunk("far")
    ring_c.far()

    pack_state(stb, q, [ngh, ngl],
               jnp.sum(dg[...] * q[...].astype(f32), axis=0, keepdims=True))
    state = State(stb, b0, b1, b2, bfin, bsum)
    state.step0()
    out_chunk("right")
    ring_c.near_right()
    out_chunk("left")
    ring_c.near_left()
    state.step1()

    def pack(r, one, two, rows):
        t1 = one[:, 512:WP].astype(f32)
        t2 = two[:, 512:WP].astype(f32)
        tail = t1 + pltpu.roll(t2, 48, 1)
        send[r, 0:512] = one[:, 0:512].astype(f32)
        send[r, 512:1024] = two[:, 0:512].astype(f32)
        send[r, 1024:GC] = tail
        rhs[r, 0:512] = one[:, 0:512]
        rhs[r, 512:1024] = two[:, 0:512]
        rhs[r, 1024:GC] = tail.astype(bf16)

    def query_grad(i):
        r = pl.ds(pl.multiple_of(i * 128, 128), 128)
        high, low = ngh[r, :], ngl[r, :]
        value = dot_t(high, kvh[...]) + dot_t(high, kvl[...]) + dot_t(low, kvh[...])
        value = value + dg[r, :] * ksum
        value = jnp.where(q[r, :].astype(f32) > 0, value, 0.0).astype(bf16)
        gm[r, :] = value
        pack(r, mx[r, :], value, 128)

    loop(T // 128, query_grad)
    dq = gm
    pair = copies.start(send, recv, partner)
    state.step2()

    def cast_rows(dst, base):
        def cast(i):
            r = pl.multiple_of(i * 288, 16)
            dst[pl.ds(r, 288), T:2 * T] = dp[pl.ds(pl.multiple_of(base + r, 8), 288), :].astype(bf16)

        loop(GR // 288, cast)

    cast_rows(tokt, 0)
    cast_rows(got, GR)
    out_chunk("own")
    state.step3()

    def take_pair():
        def cast(i):
            r = pl.multiple_of(i * 128, 128)
            rhs[pl.ds(T + r, 128), :] = recv[pl.ds(r, 128), :].astype(bf16)

        loop(T // 128, cast)

    pair.wait_recv()
    take_pair()
    copies.sent(pair)

    ring_f = {"far": (fa + 2) % 4, "right": (fa + 1) % 4, "left": (fa + 3) % 4, "own": fa}
    lane = functools.partial(lax.broadcasted_iota, jnp.int32, (2 * T, 128), 1)

    def place_of(which, i):
        return pl.ds(order[which] * CH + i * 144, 144) if which != "own" else pl.ds(i * 144, 144)

    def first_pair(which):
        dst = own1 if which == "own" else gbuf
        base = 0 if which == "own" else order[which] * CH

        def tile(i):
            rows = pl.ds(pl.multiple_of(ring_f[which] * CH + i * 144, 16), 144)
            to = pl.ds(pl.multiple_of(base + i * 144, 16), 144)
            lo, lt = got[rows, :], tokt[rows, :]
            tail = rhs[:, 1024:GC].astype(f32)
            tail1 = jnp.where(lane() < 48, tail, 0.0).astype(bf16)
            tail2 = jnp.where(lane() < 48, 0.0, tail).astype(bf16)
            dst[to, 0:512] = dot(lo, rhs[:, 0:512])
            dst[to, 512:1024] = dot(lt, rhs[:, 512:1024])
            dst[to, 1024:GC] = dot(lo, tail1) + dot(lt, tail2)

        loop(2, tile)

    def second_pair(which):
        dst = own2 if which == "own" else gbuf
        base = 0 if which == "own" else order[which] * CH

        def tile(i):
            rows = pl.ds(pl.multiple_of(ring_f[which] * CH + i * 144, 16), 144)
            to = pl.ds(pl.multiple_of(base + i * 144, 16), 144)
            dst[to, :] = dot(tokt[rows, :], rhs[...])

        loop(2, tile)

    def g_slot(which, h):
        return gbuf.at[pl.ds(order[which] * CH + h * 144, 144), :]

    def p_slot(buf):
        far = {"far": (sa + 2) % 4, "right": (sa + 1) % 4, "left": (sa + 3) % 4}

        def slot(which, h):
            base = far[which] * RP
            if h == 0:
                return buf.at[pl.ds(pl.multiple_of(base, 8), 40), :]
            return buf.at[pl.ds(pl.multiple_of(base + 40, 8), 32), :]

        return slot

    fr, fl = first((fa + 1) % 4), first((fa + 3) % 4)
    sr, sl = second((sa + 1) % 4), second((sa + 3) % 4)
    ring_1 = Ring(copies, fl, fr, g_slot, box1, 144)
    ring_2 = Ring(copies, fl, fr, g_slot, box2, 144)
    ring_p = Ring(copies, sl, sr, p_slot(own1), pbox1, 40)
    ring_r = Ring(copies, sl, sr, p_slot(own2), pbox2, 40)

    first_pair("far")
    ring_1.far()
    first_pair("right")
    ring_1.near_right()
    first_pair("left")
    ring_1.near_left()
    state.step4()
    ring_c.combine()
    first_pair("own")

    state.done()
    unpack_state(bfin)
    gsum = sums_row(bfin)
    dk, dv = ngh, ngl

    def key_value_grad(i):
        r = pl.ds(pl.multiple_of(i * 128, 128), 128)
        kt, vt = k[r, :], v[r, :]
        one = dot_t(vt, kvh[...]) + dot_t(vt, kvl[...]) + gsum
        one = jnp.where(kt.astype(f32) > 0, one, 0.0).astype(bf16)
        two = (dot(kt, kvh[...]) + dot(kt, kvl[...])).astype(bf16)
        dk[r, :] = one
        dv[r, :] = two
        pack(r, one, two, 128)

    loop(T // 128, key_value_grad)
    pair = copies.start(send, recv, partner)

    def in_chunk(which, place):
        def part(i, grad):
            return dot_t(wslot[place, W * i:W * i + W, :], grad[:, 0:W])

        dp[pl.ds(order[which] * W, W), :] = part(0, dq) + part(1, dk) + part(2, dv)

    ring_d = Ring(copies, down, up, y_slot(dp), dbox, W // 2)
    for copy in fetch_far:
        copy.wait()
    in_chunk("far", 0)
    ring_d.far()
    fetch_left = fetch("left", 0)
    ring_1.combine()
    for copy in fetch_right:
        copy.wait()
    in_chunk("right", 1)
    ring_d.near_right()
    fetch_own = fetch("own", 1)
    for copy in fetch_left:
        copy.wait()
    in_chunk("left", 0)
    ring_d.near_left()

    pair.wait_recv()
    take_pair()
    ring_1.sent(("a0", "a1"))
    second_pair("far")
    ring_2.far()
    second_pair("own")
    for copy in fetch_own:
        copy.wait()
    in_chunk("own", 1)

    ring_1.sent(("d0", "d1", "c0", "c1"))
    second_pair("right")
    ring_2.near_right()
    second_pair("left")
    ring_2.near_left()

    def add_up(dst, box, rows, tile):
        def step(i):
            r = pl.ds(pl.multiple_of(i * tile, 8), tile)
            dst[r, :] = dst[r, :] + (box[1, r, :] + box[2, r, :])

        loop(rows // tile, step)

    ring_1.arrived()
    add_up(own1, box1, CH, 96)
    ring_p.far()
    ring_p.near_right()
    ring_p.near_left()

    ring_c.arrived()

    def attn_sum(i):
        r = pl.multiple_of(i * 112, 8)
        at = pl.ds(pl.multiple_of(3 * W + r, 8), 112)
        rb = pl.ds(r, 112)
        cp[at, :] = cp[at, :] + (cbox[1, rb, :] + cbox[2, rb, :])

    loop(W // 112, attn_sum)
    out_c = local(cp.at[pl.ds(3 * W, W), :], at_o, out_sem.at[0])

    ring_2.combine()
    ring_p.combine()
    ring_d.combine()

    def final(src, box, out, sem):
        rows = pl.ds(pl.multiple_of(sa * RP, 8), RP)
        src[rows, :] = src[rows, :] + (box[1] + box[2])
        return local(src.at[rows, :], out, sem)

    ring_p.arrived()
    out_1 = final(own1, pbox1, g1_o, out_sem.at[1])

    ring_2.arrived()
    add_up(own2, box2, CH, 96)
    ring_r.far()
    ring_r.near_right()
    ring_r.near_left()
    ring_r.combine()
    ring_r.arrived()
    out_2 = final(own2, pbox2, g2_o, out_sem.at[2])

    ring_d.arrived()

    def tok_sum(i):
        r = pl.multiple_of(i * 112, 8)
        at = pl.ds(pl.multiple_of(3 * W + r, 8), 112)
        rb = pl.ds(r, 112)
        dp[at, :] = dp[at, :] + (dbox[1, rb, :] + dbox[2, rb, :])

    loop(W // 112, tok_sum)
    out_d = local(dp.at[pl.ds(3 * W, W), :], gt_o, out_sem.at[3])
    copies.finish()
    for copy in (out_c, out_1, out_2, out_d):
        copy.wait()


def body(tokens, w_query, w_key, w_value, w_out, grad_out):
    shapes = [
        ((T, D), bf16), ((T, D), bf16), ((2, D, W), bf16), ((W, D), bf16), ((D, W), bf16),
        ((GR, 2 * T), bf16), ((GR, 2 * T), bf16),
        ((T, WP), bf16), ((T, WP), bf16), ((T, WP), bf16), ((T, WP), bf16), ((T, WP), bf16),
        ((T, WP), bf16), ((T, WP), bf16), ((T, WP), f32),
        ((WP, WP), bf16), ((WP, WP), bf16), ((WP, WP), bf16),
        ((T, GC), f32), ((T, GC), f32), ((2 * T, GC), bf16),
        ((3 * CH, GC), f32), ((CH, GC), f32), ((CH, GC), f32),
        ((3, CH, GC), f32), ((3, CH, GC), f32), ((3, RP, GC), f32), ((3, RP, GC), f32),
        ((2 * GR, T), f32), ((2 * GR, T), f32), ((3, W, T), f32), ((3, W, T), f32),
    ]
    for _ in range(2):
        shapes += [((SR, 128), f32), ((SR // 2, 128), f32), ((3, RP, 128), f32), ((3, RP, 128), f32),
                   ((SR, 128), f32), ((RP, 128), f32)]
    scratch = [pltpu.VMEM(*shape) for shape in shapes]
    scratch += [
        pltpu.SemaphoreType.DMA((6,)), pltpu.SemaphoreType.DMA((2, 3)), pltpu.SemaphoreType.DMA((4,)),
        pltpu.SemaphoreType.DMA((64,)), pltpu.SemaphoreType.DMA((64,)),
    ]
    at, gt, g1, g2 = pl.pallas_call(
        kernel,
        out_shape=(
            jax.ShapeDtypeStruct((W, T), f32), jax.ShapeDtypeStruct((W, T), f32),
            jax.ShapeDtypeStruct((RP, GC), f32), jax.ShapeDtypeStruct((RP, GC), f32),
        ),
        in_specs=[pl.BlockSpec(memory_space=pl.ANY)] * 6,
        out_specs=[pl.BlockSpec(memory_space=pl.ANY)] * 4,
        scratch_shapes=scratch,
        compiler_params=pltpu.CompilerParams(
            collective_id=0, has_side_effects=True, vmem_limit_bytes=64 * 1024 * 1024 - 65536),
        cost_estimate=pl.CostEstimate(flops=16 * 10**9, bytes_accessed=16 * 10**6, transcendentals=0),
        name="fused_attention",
    )(tokens, w_query, w_key, w_value, w_out, grad_out)
    factor = 1.0 / math.sqrt(T * lax.axis_size("seq"))
    g1 = g1[:ROWS] * factor
    g2 = g2[:ROWS] * factor

    def one(g):
        return jnp.concatenate([g[:, 0:512], g[:, 1024:1072]], axis=1)

    def two(g):
        return jnp.concatenate([g[:, 512:1024], g[:, 1072:1120]], axis=1)

    return (at.T.astype(bf16), gt.T.astype(bf16), two(g1), one(g2), two(g2), one(g1).T)


def solution(mesh):
    in_specs = (
        P("seq", None),
        P(None, "head"),
        P(None, "head"),
        P(None, "head"),
        P("head", None),
        P("seq", None),
    )
    out_specs = (
        P("seq", "head"),
        P("seq", "head"),
        P("seq", "head"),
        P("seq", "head"),
        P("seq", "head"),
        P("head", "seq"),
    )
    return jax.shard_map(body, mesh=mesh, in_specs=in_specs, out_specs=out_specs, check_vma=False)
```

```python
import functools
import math

import jax
import jax.numpy as jnp
from jax import lax
from jax.experimental import pallas as pl
from jax.experimental.pallas import tpu as pltpu
from jax.sharding import PartitionSpec as P

f32 = jnp.float32
bf16 = jnp.bfloat16
MESH = pl.DeviceIdType.MESH

D = 2240
W = 560
HEADS = 5
HP = 128
T = 384
HD = 112
ROWS = 70
RP = 72
NB = 16
GR = NB * RP
GC = 1152
CH = 4 * RP
SR = 576
EPS = 1e-15


def dot(a, b):
    return lax.dot_general(a, b, (((1,), (0,)), ((), ())), preferred_element_type=f32)


def dot_t(a, b):
    return lax.dot_general(a, b, (((1,), (1,)), ((), ())), preferred_element_type=f32)


def dot_n(a, b):
    return lax.dot_general(a, b, (((0,), (0,)), ((), ())), preferred_element_type=f32)


def parts(v):
    high = v.astype(bf16)
    return high, (v - high.astype(f32)).astype(bf16)


def loop(count, fn):
    def step(i, carry):
        fn(i)
        return carry

    lax.fori_loop(0, count, step, 0)


class Copies:
    def __init__(self, send, recv):
        self.send, self.recv, self.used, self.open = send, recv, 0, []

    def start(self, src, dst, device):
        k = self.used
        self.used += 1
        copy = pltpu.make_async_remote_copy(
            src_ref=src, dst_ref=dst, send_sem=self.send.at[k], recv_sem=self.recv.at[k],
            device_id=device, device_id_type=MESH)
        copy.start()
        self.open.append(copy)
        return copy

    def sent(self, copy):
        copy.wait_send()
        self.open = [other for other in self.open if other is not copy]

    def finish(self):
        for copy in self.open:
            copy.wait_send()
        self.open = []


class Ring:
    def __init__(self, copies, left, right, slot, box, cut):
        self.copies, self.left, self.right, self.slot = copies, left, right, slot
        self.box, self.cut = box, cut
        self.rows = box.shape[1]

    def land(self, kind, half):
        if half == 0:
            return self.box.at[kind, pl.ds(0, self.cut), :]
        return self.box.at[kind, pl.ds(self.cut, self.rows - self.cut), :]

    def far(self):
        self.a0 = self.copies.start(self.slot("far", 0), self.land(0, 0), self.right)
        self.a1 = self.copies.start(self.slot("far", 1), self.land(0, 1), self.left)

    def near_right(self):
        self.d1 = self.copies.start(self.slot("right", 1), self.land(1, 1), self.right)

    def near_left(self):
        self.d0 = self.copies.start(self.slot("left", 0), self.land(1, 0), self.left)

    def combine(self):
        self.a0.wait_recv()
        ref = self.slot("right", 0)
        ref[...] = ref[...] + self.land(0, 0)[...]
        self.c0 = self.copies.start(ref, self.land(2, 0), self.right)
        self.a1.wait_recv()
        ref = self.slot("left", 1)
        ref[...] = ref[...] + self.land(0, 1)[...]
        self.c1 = self.copies.start(ref, self.land(2, 1), self.left)

    def arrived(self):
        for copy in (self.d0, self.d1, self.c0, self.c1):
            copy.wait_recv()

    def sent(self, names):
        for name in names:
            self.copies.sent(getattr(self, name))


def kernel(tok_h, wq_h, wk_h, wv_h, wo_h, go_h,
           at_o, gt_o, g1_o, g2_o,
           tok, go, wslot, wot, wqn, wkn, wvn, tokt, got,
           q, k, v, gm, ngh, ngl, rhs1, rhs2, send, recv,
           gbuf, own1, own2, box1, box2, pbox1, pbox2,
           cp, dp, cbox, dbox,
           sta, a0, a1, a2, afin, asum, stb, b0, b1, b2, bfin, bsum,
           in_sem, out_sem, ssem, rsem):
    s = lax.axis_index("seq")
    y = lax.axis_index("head")
    c = s % 2
    chip = s // 2
    x = chip // 4
    z = chip % 4
    fa = x * (1 - c) + z * c
    sa = z * (1 - c) + x * c

    def first(i):
        return {"seq": ((i * (1 - c) + sa * c) * 4 + sa * (1 - c) + i * c) * 2 + c, "head": y}

    def second(i):
        return {"seq": ((fa * (1 - c) + i * c) * 4 + i * (1 - c) + fa * c) * 2 + c, "head": y}

    def along_y(i):
        return {"seq": s, "head": i}

    partner = {"seq": s + 1 - 2 * c, "head": y}

    def local(src, dst, sem):
        copy = pltpu.make_async_copy(src, dst, sem)
        copy.start()
        return copy

    in_tok = local(tok_h, tok, in_sem.at[0])
    in_k = local(wk_h, wslot.at[0], in_sem.at[1])
    in_v = local(wv_h, wslot.at[1], in_sem.at[2])
    in_go = local(go_h, go, in_sem.at[3])

    barrier = pltpu.get_barrier_semaphore()
    peers = [partner, along_y((y + 1) % 4), along_y((y + 3) % 4)]
    peers += [first((fa + d) % 4) for d in (1, 2, 3)]
    peers += [second((sa + d) % 4) for d in (1, 2, 3)]
    for peer in peers:
        pl.semaphore_signal(barrier, inc=1, device_id=peer, device_id_type=MESH)

    copies = Copies(ssem, rsem)

    def head(h):
        return pl.ds(pl.multiple_of(h * HD, 16), HD)

    def block(h):
        return pl.ds(pl.multiple_of(h * HP, HP), HP)

    def sum_row(row):
        keep = lax.broadcasted_iota(jnp.int32, (HP - HD, T), 0) == 0
        return jnp.where(keep, row, 0.0)

    def state_part(st, left, rights):
        def one(h):
            total = None
            for right in rights:
                value = dot_t(left[head(h), :], right[block(h), :])
                total = value if total is None else total + value
            st[head(h), :] = total

        loop(HEADS, one)
        st[W:SR, :] = jnp.zeros((SR - W, HP), f32)

    half = SR // 2
    piece = half // 4
    mine = pl.multiple_of(c * half, 8)
    other = pl.multiple_of((1 - c) * half, 8)

    def mine_piece(i):
        return pl.ds(pl.multiple_of(c * half + i * piece, 8), piece)

    class State:
        def __init__(self, st, r0, r1, r2, fin, total):
            self.st, self.r0, self.r1, self.r2, self.fin, self.total = st, r0, r1, r2, fin, total

        def step0(self):
            self.c = copies.start(self.st.at[pl.ds(other, half), :], self.r0, partner)

        def step1(self):
            self.c.wait_recv()
            rows = pl.ds(mine, half)
            self.st[rows, :] = self.st[rows, :] + self.r0[...]
            self.cs = [copies.start(self.st.at[mine_piece((fa + d) % 4), :], self.r1.at[d - 1],
                                    first((fa + d) % 4)) for d in (1, 2, 3)]

        def step2(self):
            for copy in self.cs:
                copy.wait_recv()
            self.total[...] = (self.st[mine_piece(fa), :] + self.r1[0]) + (self.r1[1] + self.r1[2])
            self.cs = [copies.start(self.total, self.r2.at[d - 1], second((sa + d) % 4))
                       for d in (1, 2, 3)]

        def step3(self):
            for copy in self.cs:
                copy.wait_recv()
            rows = mine_piece(fa)
            self.fin[rows, :] = (self.total[...] + self.r2[0]) + (self.r2[1] + self.r2[2])
            self.cs = [copies.start(self.fin.at[rows, :], self.fin.at[rows, :], first((fa + d) % 4))
                       for d in (1, 2, 3)]

        def step4(self):
            for copy in self.cs:
                copy.wait_recv()
            rows = pl.ds(mine, half)
            self.c = copies.start(self.fin.at[rows, :], self.fin.at[rows, :], partner)

        def done(self):
            self.c.wait_recv()

    in_tok.wait()
    in_k.wait()
    k[...] = jnp.maximum(dot(wslot[0], tok[...]), 0.0).astype(bf16)
    in_q = local(wq_h, wslot.at[0], in_sem.at[4])
    in_v.wait()
    value = dot(wslot[1], tok[...]).astype(bf16)
    for h in range(HEADS):
        v[HP * h:HP * h + HD, :] = value[HD * h:HD * h + HD, :]
        v[HP * h + HD:HP * h + HP, :] = sum_row(jnp.ones((1, T), f32)).astype(bf16)
    in_o = local(wo_h, wslot.at[1], in_sem.at[5])
    state_part(sta, k, [v])
    pl.semaphore_wait(barrier, len(peers))
    state = State(sta, a0, a1, a2, afin, asum)
    state.step0()

    in_q.wait()
    q[...] = jnp.maximum(dot(wslot[0], tok[...]), 0.0).astype(bf16)
    state.step1()

    def gather_rows(src, base, which):
        for b in range(NB):
            lo = 2 * ROWS * b
            w0 = lo // 16 * 16
            w1 = -(-(lo + 2 * ROWS) // 16) * 16
            i = lax.broadcasted_iota(jnp.int32, (RP, w1 - w0), 0)
            j = lax.broadcasted_iota(jnp.int32, (RP, w1 - w0), 1)
            pick = jnp.logical_and(j == i + (lo - w0) + ROWS * which, i < ROWS)
            place = b * (1 - which) + (b % 4 * 4 + b // 4) * which
            cp[pl.ds(pl.multiple_of(base + place * RP, 8), RP), :] = dot(
                pick.astype(f32).astype(bf16), src[w0:w1, :])

    def rows_of(src, dst, base):
        gather_rows(src, base, c)

        def cast(i):
            r = pl.multiple_of(i * 288, 16)
            dst[pl.ds(r, 288), 0:T] = cp[pl.ds(pl.multiple_of(base + r, 8), 288), :].astype(bf16)

        loop(GR // 288, cast)
        gather_rows(src, base, 1 - c)
        place = pl.ds(base, GR)
        return copies.start(cp.at[place, :], dp.at[place, :], partner)

    def flip(src, dst):
        def columns(start, n):
            eye = (lax.broadcasted_iota(jnp.int32, (n, n), 0) == lax.broadcasted_iota(jnp.int32, (n, n), 1))
            dst[pl.ds(start, n), :] = dot_t(
                eye.astype(f32).astype(bf16), src[:, pl.ds(start, n)]).astype(bf16)

        loop(D // 256, lambda i: columns(pl.multiple_of(i * 256, 256), 256))
        columns(D // 256 * 256, D % 256)

    send_tok = rows_of(tok, tokt, 0)
    state.step2()

    in_o.wait()
    in_go.wait()
    gm[...] = dot(wslot[1], go[...]).astype(bf16)
    state.step3()
    send_go = rows_of(go, got, GR)
    state.step4()
    flip(wslot.at[1], wot)
    in_v = local(wv_h, wslot.at[1], in_sem.at[2])
    rhs1[2 * W:GC, :] = jnp.zeros((GC - 2 * W, 2 * T), bf16)
    rhs2[2 * W:GC, :] = jnp.zeros((GC - 2 * W, 2 * T), bf16)

    state.done()

    def attend(h):
        high, low = parts(afin[head(h), :])
        qt = q[head(h), :]
        both = dot_n(high, qt) + dot_n(low, qt)
        rec = 1.0 / (both[HD:HD + 1, :] + EPS)
        att = both[0:HD, :] * rec
        rhs1[head(h), 0:T] = att.astype(bf16)
        send[head(h), :] = att.astype(bf16).astype(f32)
        g = gm[head(h), :].astype(f32)
        grad = -jnp.sum(g * att, axis=0, keepdims=True) * rec
        high, low = parts(g * rec)
        at = pl.ds(pl.multiple_of(h * HP, HP), HD)
        ngh[at, :] = high
        ngl[at, :] = low
        high, low = parts(sum_row(grad))
        at = pl.ds(pl.multiple_of(h * HP + HD, 16), HP - HD)
        ngh[at, :] = high
        ngl[at, :] = low

    loop(HEADS, attend)

    ring_y = {"far": (y + 2) % 4, "right": (y + 1) % 4, "left": (y + 3) % 4, "own": y}
    order = {"far": 0, "right": 1, "left": 2, "own": 3}
    copies.sent(send_tok)
    copies.sent(send_go)

    def y_rows(which):
        return pl.ds(pl.multiple_of(ring_y[which] * W, 16), W)

    def out_chunk(which):
        cp[pl.ds(order[which] * W, W), :] = dot(wot[y_rows(which), :], rhs1[0:W, 0:T])

    def y_slot(buf):
        def slot(which, h):
            return buf.at[pl.ds(order[which] * W + h * (W // 2), W // 2), :]

        return slot

    up, down = along_y((y + 1) % 4), along_y((y + 3) % 4)
    ring_c = Ring(copies, down, up, y_slot(cp), cbox, W // 2)
    out_chunk("far")
    ring_c.far()

    state_part(stb, q, [ngh, ngl])
    state = State(stb, b0, b1, b2, bfin, bsum)
    state.step0()
    out_chunk("right")
    ring_c.near_right()
    out_chunk("left")
    ring_c.near_left()
    state.step1()

    def query_grad(h):
        high, low = parts(afin[head(h), :])
        ng = ngh[block(h), :]
        value = dot(high, ng) + dot(low, ng) + dot(high, ngl[block(h), :])
        value = jnp.where(q[head(h), :].astype(f32) > 0, value, 0.0).astype(bf16)
        at = pl.ds(pl.multiple_of(W + h * HD, 16), HD)
        rhs1[at, 0:T] = value
        send[at, :] = value.astype(f32)

    loop(HEADS, query_grad)
    pair = copies.start(send, recv, partner)
    state.step2()

    def cast_rows(dst, base):
        def cast(i):
            r = pl.multiple_of(i * 288, 16)
            dst[pl.ds(r, 288), T:2 * T] = dp[pl.ds(pl.multiple_of(base + r, 8), 288), :].astype(bf16)

        loop(GR // 288, cast)

    flip(wslot.at[0], wqn)
    in_k = local(wk_h, wslot.at[0], in_sem.at[1])
    send_tok.wait_recv()
    cast_rows(tokt, 0)
    send_go.wait_recv()
    cast_rows(got, GR)
    state.step3()

    def take_pair(dst):
        def cast(i):
            r = pl.ds(pl.multiple_of(i * HD, 16), HD)
            dst[r, T:2 * T] = recv[r, :].astype(bf16)

        loop(2 * W // HD, cast)

    pair.wait_recv()
    take_pair(rhs1)
    copies.sent(pair)

    ring_f = {"far": (fa + 2) % 4, "right": (fa + 1) % 4, "left": (fa + 3) % 4, "own": fa}

    def tiles_of(which, dst, fn):
        base = 0 if which == "own" else order[which] * CH

        def tile(i):
            rows = pl.ds(pl.multiple_of(ring_f[which] * CH + i * 144, 16), 144)
            fn(rows, dst, pl.ds(pl.multiple_of(base + i * 144, 16), 144))

        loop(2, tile)

    def first_tile(rows, dst, to):
        lo, lt = got[rows, :], tokt[rows, :]
        dst[to, 0:512] = dot_t(lo, rhs1[0:512, :])
        shared = rhs1[512:640, :]
        is_out = lax.broadcasted_iota(jnp.int32, (144, 128), 1) < W - 512
        dst[to, 512:640] = jnp.where(is_out, dot_t(lo, shared), dot_t(lt, shared))
        dst[to, 640:GC] = dot_t(lt, rhs1[640:GC, :])

    def second_tile(rows, dst, to):
        dst[to, :] = dot_t(tokt[rows, :], rhs2[...])

    def first_pair(which):
        tiles_of(which, own1 if which == "own" else gbuf, first_tile)

    def second_pair(which):
        tiles_of(which, own2 if which == "own" else gbuf, second_tile)

    def g_slot(which, h):
        return gbuf.at[pl.ds(order[which] * CH + h * 144, 144), :]

    def p_slot(buf):
        far = {"far": (sa + 2) % 4, "right": (sa + 1) % 4, "left": (sa + 3) % 4}

        def slot(which, h):
            base = far[which] * RP
            if h == 0:
                return buf.at[pl.ds(pl.multiple_of(base, 8), 40), :]
            return buf.at[pl.ds(pl.multiple_of(base + 40, 8), 32), :]

        return slot

    fr, fl = first((fa + 1) % 4), first((fa + 3) % 4)
    sr, sl = second((sa + 1) % 4), second((sa + 3) % 4)
    ring_1 = Ring(copies, fl, fr, g_slot, box1, 144)
    ring_2 = Ring(copies, fl, fr, g_slot, box2, 144)
    ring_p = Ring(copies, sl, sr, p_slot(own1), pbox1, 40)
    ring_r = Ring(copies, sl, sr, p_slot(own2), pbox2, 40)

    first_pair("far")
    ring_1.far()
    state.step4()
    first_pair("right")
    ring_1.near_right()
    first_pair("left")
    ring_1.near_left()
    ring_c.combine()
    in_v.wait()
    flip(wslot.at[1], wvn)
    in_k.wait()
    flip(wslot.at[0], wkn)

    state.done()

    def key_value_grad(h):
        high, low = parts(bfin[head(h), :])
        kt, vt = k[head(h), :], v[block(h), :]
        one = dot(high, vt) + dot(low, vt)
        one = jnp.where(kt.astype(f32) > 0, one, 0.0).astype(bf16)
        two = (dot_n(high, kt) + dot_n(low, kt))[0:HD, :].astype(bf16)
        rhs2[head(h), 0:T] = one
        send[head(h), :] = one.astype(f32)
        at = pl.ds(pl.multiple_of(W + h * HD, 16), HD)
        rhs2[at, 0:T] = two
        send[at, :] = two.astype(f32)

    loop(HEADS, key_value_grad)
    pair = copies.start(send, recv, partner)

    def in_chunk(which):
        rows = y_rows(which)
        dp[pl.ds(order[which] * W, W), :] = (
            dot(wqn[rows, :], rhs1[W:2 * W, 0:T]) + dot(wkn[rows, :], rhs2[0:W, 0:T])
            + dot(wvn[rows, :], rhs2[W:2 * W, 0:T]))

    ring_d = Ring(copies, down, up, y_slot(dp), dbox, W // 2)
    in_chunk("far")
    ring_d.far()
    ring_1.combine()
    in_chunk("right")
    ring_d.near_right()
    in_chunk("left")
    ring_d.near_left()

    pair.wait_recv()
    take_pair(rhs2)
    first_pair("own")
    ring_1.sent(("a0", "a1"))
    second_pair("far")
    ring_2.far()
    second_pair("own")
    out_chunk("own")
    in_chunk("own")

    ring_1.sent(("d0", "d1", "c0", "c1"))
    second_pair("right")
    ring_2.near_right()
    second_pair("left")
    ring_2.near_left()

    def add_up(dst, box, rows, tile):
        def step(i):
            r = pl.ds(pl.multiple_of(i * tile, 8), tile)
            dst[r, :] = dst[r, :] + (box[1, r, :] + box[2, r, :])

        loop(rows // tile, step)

    ring_1.arrived()
    add_up(own1, box1, CH, 96)
    ring_p.far()
    ring_p.near_right()
    ring_p.near_left()

    def y_sum(buf, box, dst, out, sem):
        def step(i):
            at = pl.ds(pl.multiple_of(3 * W + i * HD, 16), HD)
            rb = pl.ds(pl.multiple_of(i * HD, 16), HD)
            dst[rb, :] = (buf[at, :] + (box[1, rb, :] + box[2, rb, :])).astype(bf16)

        loop(HEADS, step)
        return local(dst, out, sem)

    ring_c.arrived()
    out_c = y_sum(cp, cbox, q, at_o, out_sem.at[0])

    ring_2.combine()
    ring_p.combine()
    ring_d.combine()

    def final(src, box, out, sem):
        rows = pl.ds(pl.multiple_of(sa * RP, 8), RP)
        src[rows, :] = src[rows, :] + (box[1] + box[2])
        return local(src.at[rows, :], out, sem)

    ring_p.arrived()
    out_1 = final(own1, pbox1, g1_o, out_sem.at[1])

    ring_2.arrived()
    add_up(own2, box2, CH, 96)
    ring_r.far()
    ring_r.near_right()
    ring_r.near_left()
    ring_r.combine()
    ring_r.arrived()
    out_2 = final(own2, pbox2, g2_o, out_sem.at[2])

    ring_d.arrived()
    out_d = y_sum(dp, dbox, gm, gt_o, out_sem.at[3])
    copies.finish()
    for copy in (out_c, out_1, out_2, out_d):
        copy.wait()


def finish(factor, at, gt, g1, g2, at_o, gt_o, gq_o, gk_o, gv_o, gw_o, sem):
    copies = [pltpu.make_async_copy(at, at_o, sem.at[0]), pltpu.make_async_copy(gt, gt_o, sem.at[1])]
    for copy in copies:
        copy.start()
    one, two = g1[0:ROWS, :] * factor, g2[0:ROWS, :] * factor
    gw_o[...] = one[:, 0:W]
    gq_o[...] = one[:, W:2 * W]
    gk_o[...] = two[:, 0:W]
    gv_o[...] = two[:, W:2 * W]
    for copy in copies:
        copy.wait()


def body(tokens, w_query, w_key, w_value, w_out, grad_out):
    shapes = [
        ((D, T), bf16), ((D, T), bf16), ((2, W, D), bf16),
        ((D, W), bf16), ((D, W), bf16), ((D, W), bf16), ((D, W), bf16),
        ((GR, 2 * T), bf16), ((GR, 2 * T), bf16),
        ((W, T), bf16), ((W, T), bf16), ((HEADS * HP, T), bf16), ((W, T), bf16),
        ((HEADS * HP, T), bf16), ((HEADS * HP, T), bf16),
        ((GC, 2 * T), bf16), ((GC, 2 * T), bf16), ((2 * W, T), f32), ((2 * W, T), f32),
        ((3 * CH, GC), f32), ((CH, GC), f32), ((CH, GC), f32),
        ((3, CH, GC), f32), ((3, CH, GC), f32), ((3, RP, GC), f32), ((3, RP, GC), f32),
        ((2 * GR, T), f32), ((2 * GR, T), f32), ((3, W, T), f32), ((3, W, T), f32),
    ]
    for _ in range(2):
        shapes += [((SR, HP), f32), ((SR // 2, HP), f32), ((3, RP, HP), f32), ((3, RP, HP), f32),
                   ((SR, HP), f32), ((RP, HP), f32)]
    scratch = [pltpu.VMEM(*shape) for shape in shapes]
    scratch += [
        pltpu.SemaphoreType.DMA((6,)), pltpu.SemaphoreType.DMA((4,)),
        pltpu.SemaphoreType.DMA((64,)), pltpu.SemaphoreType.DMA((64,)),
    ]
    spaces = [pl.BlockSpec(memory_space=pl.ANY)] * 6
    at, gt, g1, g2 = pl.pallas_call(
        kernel,
        out_shape=(
            jax.ShapeDtypeStruct((W, T), bf16), jax.ShapeDtypeStruct((W, T), bf16),
            jax.ShapeDtypeStruct((RP, GC), f32), jax.ShapeDtypeStruct((RP, GC), f32),
        ),
        in_specs=spaces,
        out_specs=spaces[:4],
        scratch_shapes=scratch,
        compiler_params=pltpu.CompilerParams(
            collective_id=0, has_side_effects=True, vmem_limit_bytes=64 * 1024 * 1024 - 65536),
        cost_estimate=pl.CostEstimate(flops=16 * 10**9, bytes_accessed=16 * 10**6, transcendentals=0),
        name="fused_attention",
    )(tokens.T, w_query.T, w_key.T, w_value.T, w_out, grad_out.T)
    factor = 1.0 / math.sqrt(T * lax.axis_size("seq"))
    grad = jax.ShapeDtypeStruct((ROWS, W), f32)
    vmem = pl.BlockSpec(memory_space=pltpu.VMEM)
    at, gt, gq, gk, gv, gw = pl.pallas_call(
        functools.partial(finish, factor),
        out_shape=(
            jax.ShapeDtypeStruct((W, T), bf16), jax.ShapeDtypeStruct((W, T), bf16),
            grad, grad, grad, grad,
        ),
        in_specs=spaces[:2] + [vmem] * 2,
        out_specs=spaces[:2] + [vmem] * 4,
        scratch_shapes=[pltpu.SemaphoreType.DMA((2,))],
        name="final_arrays",
    )(at, gt, g1, g2)
    return (at.T, gt.T, gq, gk, gv, gw.T)


def solution(mesh):
    in_specs = (
        P("seq", None),
        P(None, "head"),
        P(None, "head"),
        P(None, "head"),
        P("head", None),
        P("seq", None),
    )
    out_specs = (
        P("seq", "head"),
        P("seq", "head"),
        P("seq", "head"),
        P("seq", "head"),
        P("seq", "head"),
        P("head", "seq"),
    )
    return jax.shard_map(body, mesh=mesh, in_specs=in_specs, out_specs=out_specs, check_vma=False)
```

```python
import functools
import math

import jax
import jax.numpy as jnp
from jax import lax
from jax.experimental import pallas as pl
from jax.experimental.pallas import tpu as pltpu
from jax.sharding import PartitionSpec as P

f32 = jnp.float32
bf16 = jnp.bfloat16
MESH = pl.DeviceIdType.MESH

D = 2240
W = 560
HEADS = 5
HP = 128
T = 384
HD = 112
ROWS = 70
RP = 72
NB = 16
GR = NB * RP
GC = 1152
CH = 4 * RP
PR = 24
SR = 2 * NB * PR
EPS = 1e-15


def dot(a, b):
    return lax.dot_general(a, b, (((1,), (0,)), ((), ())), preferred_element_type=f32)


def dot_t(a, b):
    return lax.dot_general(a, b, (((1,), (1,)), ((), ())), preferred_element_type=f32)


def dot_n(a, b):
    return lax.dot_general(a, b, (((0,), (0,)), ((), ())), preferred_element_type=f32)


def parts(v):
    high = v.astype(bf16)
    return high, (v - high.astype(f32)).astype(bf16)


def each(count, fn):
    for i in range(count):
        fn(i)


def loop(count, fn):
    def step(i, carry):
        fn(i)
        return carry

    lax.fori_loop(0, count, step, 0)


class Copies:
    def __init__(self, send, recv):
        self.send, self.recv, self.used, self.open = send, recv, 0, []

    def start(self, src, dst, device):
        k = self.used
        self.used += 1
        copy = pltpu.make_async_remote_copy(
            src_ref=src, dst_ref=dst, send_sem=self.send.at[k], recv_sem=self.recv.at[k],
            device_id=device, device_id_type=MESH)
        copy.start()
        self.open.append(copy)
        return copy

    def sent(self, copy):
        copy.wait_send()
        self.open = [other for other in self.open if other is not copy]

    def finish(self):
        for copy in self.open:
            copy.wait_send()
        self.open = []


class Ring:
    def __init__(self, copies, left, right, slot, box, cut):
        self.copies, self.left, self.right, self.slot = copies, left, right, slot
        self.box, self.cut = box, cut
        self.rows = box.shape[1]

    def land(self, kind, half):
        if half == 0:
            return self.box.at[kind, pl.ds(0, self.cut), :]
        return self.box.at[kind, pl.ds(self.cut, self.rows - self.cut), :]

    def far(self):
        self.a0 = self.copies.start(self.slot("far", 0), self.land(0, 0), self.right)
        self.a1 = self.copies.start(self.slot("far", 1), self.land(0, 1), self.left)

    def near_right(self):
        self.d1 = self.copies.start(self.slot("right", 1), self.land(1, 1), self.right)

    def near_left(self):
        self.d0 = self.copies.start(self.slot("left", 0), self.land(1, 0), self.left)

    def combine(self):
        self.a0.wait_recv()
        ref = self.slot("right", 0)
        ref[...] = ref[...] + self.land(0, 0)[...]
        self.c0 = self.copies.start(ref, self.land(2, 0), self.right)
        self.a1.wait_recv()
        ref = self.slot("left", 1)
        ref[...] = ref[...] + self.land(0, 1)[...]
        self.c1 = self.copies.start(ref, self.land(2, 1), self.left)

    def arrived(self):
        for copy in (self.d0, self.d1, self.c0, self.c1):
            copy.wait_recv()

    def sent(self, names):
        for name in names:
            self.copies.sent(getattr(self, name))


def kernel(tok_h, wq_h, wk_h, wv_h, wo_h, go_h,
           at_o, gt_o, g1_o, g2_o,
           tok, go, wslot, wot, wqn, wkn, wvn, tokt, got,
           q, k, v, gm, ngh, ngl, rhs1, rhs2, send, recv,
           gbuf, own1, own2, box1, box2, pbox1, pbox2,
           cp, dp, cbox, dbox,
           sta, a0, a1, afin, stb, b0, b1, bfin,
           in_sem, out_sem, ssem, rsem):
    s = lax.axis_index("seq")
    y = lax.axis_index("head")
    c = s % 2
    chip = s // 2
    x = chip // 4
    z = chip % 4
    fa = x * (1 - c) + z * c
    sa = z * (1 - c) + x * c

    def first(i):
        return {"seq": ((i * (1 - c) + sa * c) * 4 + sa * (1 - c) + i * c) * 2 + c, "head": y}

    def second(i):
        return {"seq": ((fa * (1 - c) + i * c) * 4 + i * (1 - c) + fa * c) * 2 + c, "head": y}

    def along_y(i):
        return {"seq": s, "head": i}

    def chip_at(dx, dz):
        return {"seq": ((x + dx) % 4 * 4 + (z + dz) % 4) * 2 + c, "head": y}

    others = sorted([(dx, dz) for dx in range(4) for dz in range(4) if dx or dz],
                    key=lambda place: -sum(min(d, 4 - d) for d in place))
    partner = {"seq": s + 1 - 2 * c, "head": y}

    def local(src, dst, sem):
        copy = pltpu.make_async_copy(src, dst, sem)
        copy.start()
        return copy

    in_tok = local(tok_h, tok, in_sem.at[0])
    in_k = local(wk_h, wslot.at[0], in_sem.at[1])
    in_v = local(wv_h, wslot.at[1], in_sem.at[2])
    in_go = local(go_h, go, in_sem.at[3])

    barrier = pltpu.get_barrier_semaphore()
    peers = [partner, along_y((y + 1) % 4), along_y((y + 3) % 4)]
    peers += [chip_at(*place) for place in others]
    for peer in peers:
        pl.semaphore_signal(barrier, inc=1, device_id=peer, device_id_type=MESH)

    copies = Copies(ssem, rsem)

    def head(h):
        return pl.ds(h * HD, HD)

    def block(h):
        return pl.ds(h * HP, HP)

    def sum_row(row):
        keep = lax.broadcasted_iota(jnp.int32, (HP - HD, T), 0) == 0
        return jnp.where(keep, row, 0.0)

    def state_part(st, left, rights):
        def one(h):
            total = None
            for right in rights:
                value = dot_t(left[head(h), :], right[block(h), :])
                total = value if total is None else total + value
            st[head(h), :] = total

        each(HEADS, one)
        st[W:SR, :] = jnp.zeros((SR - W, HP), f32)

    half = SR // 2
    mine = pl.multiple_of(c * half, 8)
    other = pl.multiple_of((1 - c) * half, 8)

    def piece(dx, dz):
        place = (x + dx) % 4 * 4 + (z + dz) % 4
        return pl.ds(pl.multiple_of(c * half + place * PR, 8), PR)

    class State:
        def __init__(self, st, r0, r1, fin):
            self.st, self.r0, self.r1, self.fin = st, r0, r1, fin

        def step0(self):
            self.c = copies.start(self.st.at[pl.ds(other, half), :], self.r0, partner)

        def step1(self):
            self.c.wait_recv()
            rows = pl.ds(mine, half)
            self.st[rows, :] = self.st[rows, :] + self.r0[...]
            self.cs = [copies.start(self.st.at[piece(*place), :], self.r1.at[i], chip_at(*place))
                       for i, place in enumerate(others)]

        def step2(self):
            for copy in self.cs:
                copy.wait_recv()
            rows = piece(0, 0)
            total = self.st[rows, :]
            for i in range(0, NB - 1, 3):
                total = total + (self.r1[i] + self.r1[i + 1] + self.r1[i + 2])
            self.fin[rows, :] = total
            self.cs = [copies.start(self.fin.at[rows, :], self.fin.at[rows, :], chip_at(*place))
                       for place in others]

        def step3(self):
            for copy in self.cs:
                copy.wait_recv()
            rows = pl.ds(mine, half)
            self.c = copies.start(self.fin.at[rows, :], self.fin.at[rows, :], partner)

        def done(self):
            self.c.wait_recv()

    in_tok.wait()
    in_k.wait()
    k[...] = jnp.maximum(dot(wslot[0], tok[...]), 0.0).astype(bf16)
    in_q = local(wq_h, wslot.at[0], in_sem.at[4])
    in_v.wait()
    value = dot(wslot[1], tok[...]).astype(bf16)
    for h in range(HEADS):
        v[HP * h:HP * h + HD, :] = value[HD * h:HD * h + HD, :]
        v[HP * h + HD:HP * h + HP, :] = sum_row(jnp.ones((1, T), f32)).astype(bf16)
    in_o = local(wo_h, wslot.at[1], in_sem.at[5])
    state_part(sta, k, [v])
    pl.semaphore_wait(barrier, len(peers))
    state = State(sta, a0, a1, afin)
    state.step0()

    in_q.wait()
    q[...] = jnp.maximum(dot(wslot[0], tok[...]), 0.0).astype(bf16)
    state.step1()

    def gather_rows(src, base, which):
        for b in range(NB):
            lo = 2 * ROWS * b
            w0 = lo // 16 * 16
            w1 = -(-(lo + 2 * ROWS) // 16) * 16
            i = lax.broadcasted_iota(jnp.int32, (RP, w1 - w0), 0)
            j = lax.broadcasted_iota(jnp.int32, (RP, w1 - w0), 1)
            pick = jnp.logical_and(j == i + (lo - w0) + ROWS * which, i < ROWS)
            place = b * (1 - which) + (b % 4 * 4 + b // 4) * which
            cp[pl.ds(pl.multiple_of(base + place * RP, 8), RP), :] = dot(
                pick.astype(f32).astype(bf16), src[w0:w1, :])

    def rows_of(src, dst, base):
        gather_rows(src, base, c)

        def cast(i):
            r = pl.multiple_of(i * 288, 16)
            dst[pl.ds(r, 288), 0:T] = cp[pl.ds(pl.multiple_of(base + r, 8), 288), :].astype(bf16)

        loop(GR // 288, cast)
        gather_rows(src, base, 1 - c)
        place = pl.ds(base, GR)
        return copies.start(cp.at[place, :], dp.at[place, :], partner)

    def flip(src, dst):
        for start in range(0, D, 256):
            n = min(256, D - start)
            dst[start:start + n, :] = src[:, start:start + n].T

    def cast_rows(dst, base):
        def cast(i):
            r = pl.multiple_of(i * 288, 16)
            dst[pl.ds(r, 288), T:2 * T] = dp[pl.ds(pl.multiple_of(base + r, 8), 288), :].astype(bf16)

        loop(GR // 288, cast)

    send_tok = rows_of(tok, tokt, 0)
    in_o.wait()
    in_go.wait()
    gm[...] = dot(wslot[1], go[...]).astype(bf16)
    state.step2()
    send_go = rows_of(go, got, GR)
    flip(wslot.at[1], wot)
    in_v = local(wv_h, wslot.at[1], in_sem.at[2])
    send_tok.wait_recv()
    cast_rows(tokt, 0)
    state.step3()
    send_go.wait_recv()
    cast_rows(got, GR)
    flip(wslot.at[0], wqn)
    in_k = local(wk_h, wslot.at[0], in_sem.at[1])
    rhs1[2 * W:GC, :] = jnp.zeros((GC - 2 * W, 2 * T), bf16)
    rhs2[2 * W:GC, :] = jnp.zeros((GC - 2 * W, 2 * T), bf16)

    state.done()

    def attend(h):
        high, low = parts(afin[head(h), :])
        qt = q[head(h), :]
        both = dot_n(high, qt) + dot_n(low, qt)
        rec = 1.0 / (both[HD:HD + 1, :] + EPS)
        att = both[0:HD, :] * rec
        rhs1[head(h), 0:T] = att.astype(bf16)
        send[head(h), :] = att.astype(bf16).astype(f32)
        g = gm[head(h), :].astype(f32)
        grad = -jnp.sum(g * att, axis=0, keepdims=True) * rec
        high, low = parts(g * rec)
        at = pl.ds(h * HP, HD)
        ngh[at, :] = high
        ngl[at, :] = low
        high, low = parts(sum_row(grad))
        at = pl.ds(h * HP + HD, HP - HD)
        ngh[at, :] = high
        ngl[at, :] = low

    each(HEADS, attend)
    first_half, second_half = pl.ds(0, W), pl.ds(W, W)
    pair_m = copies.start(send.at[first_half, :], recv.at[first_half, :], partner)

    ring_y = {"far": (y + 2) % 4, "right": (y + 1) % 4, "left": (y + 3) % 4, "own": y}
    order = {"far": 0, "right": 1, "left": 2, "own": 3}
    copies.sent(send_tok)
    copies.sent(send_go)

    def y_rows(which):
        return pl.ds(pl.multiple_of(ring_y[which] * W, 16), W)

    def out_chunk(which):
        cp[pl.ds(order[which] * W, W), :] = dot(wot[y_rows(which), :], rhs1[0:W, 0:T])

    def y_slot(buf):
        def slot(which, h):
            return buf.at[pl.ds(order[which] * W + h * (W // 2), W // 2), :]

        return slot

    up, down = along_y((y + 1) % 4), along_y((y + 3) % 4)
    ring_c = Ring(copies, down, up, y_slot(cp), cbox, W // 2)
    out_chunk("far")
    ring_c.far()

    state_part(stb, q, [ngh, ngl])
    state = State(stb, b0, b1, bfin)
    state.step0()

    def query_grad(h):
        high, low = parts(afin[head(h), :])
        ng = ngh[block(h), :]
        value = dot(high, ng) + dot(low, ng) + dot(high, ngl[block(h), :])
        value = jnp.where(q[head(h), :].astype(f32) > 0, value, 0.0).astype(bf16)
        at = pl.ds(W + h * HD, HD)
        rhs1[at, 0:T] = value
        send[at, :] = value.astype(f32)

    each(HEADS, query_grad)
    pair_q = copies.start(send.at[second_half, :], recv.at[second_half, :], partner)
    state.step1()

    def take_pair(dst, base):
        def cast(i):
            r = pl.ds(pl.multiple_of(base + i * HD, 16), HD)
            dst[r, T:2 * T] = recv[r, :].astype(bf16)

        loop(W // HD, cast)

    pair_m.wait_recv()
    take_pair(rhs1, 0)
    pair_q.wait_recv()
    take_pair(rhs1, W)

    ring_f = {"far": (fa + 2) % 4, "right": (fa + 1) % 4, "left": (fa + 3) % 4, "own": fa}

    def chunk_of(which):
        rows = pl.ds(pl.multiple_of(ring_f[which] * CH, 16), CH)
        base = 0 if which == "own" else order[which] * CH
        return rows, pl.ds(base, CH)

    def first_pair(which):
        rows, to = chunk_of(which)
        dst = own1 if which == "own" else gbuf
        lo, lt = got[rows, :], tokt[rows, :]
        dst[to, 0:512] = dot_t(lo, rhs1[0:512, :])
        shared = rhs1[512:640, :]
        is_out = lax.broadcasted_iota(jnp.int32, (CH, 128), 1) < W - 512
        dst[to, 512:640] = jnp.where(is_out, dot_t(lo, shared), dot_t(lt, shared))
        dst[to, 640:GC] = dot_t(lt, rhs1[640:GC, :])

    def second_pair(which):
        rows, to = chunk_of(which)
        dst = own2 if which == "own" else gbuf
        dst[to, :] = dot_t(tokt[rows, :], rhs2[...])

    def g_slot(which, h):
        return gbuf.at[pl.ds(order[which] * CH + h * 144, 144), :]

    def p_slot(buf):
        far = {"far": (sa + 2) % 4, "right": (sa + 1) % 4, "left": (sa + 3) % 4}

        def slot(which, h):
            base = far[which] * RP
            if h == 0:
                return buf.at[pl.ds(pl.multiple_of(base, 8), 40), :]
            return buf.at[pl.ds(pl.multiple_of(base + 40, 8), 32), :]

        return slot

    fr, fl = first((fa + 1) % 4), first((fa + 3) % 4)
    sr, sl = second((sa + 1) % 4), second((sa + 3) % 4)
    ring_1 = Ring(copies, fl, fr, g_slot, box1, 144)
    ring_2 = Ring(copies, fl, fr, g_slot, box2, 144)
    ring_p = Ring(copies, sl, sr, p_slot(own1), pbox1, 40)
    ring_r = Ring(copies, sl, sr, p_slot(own2), pbox2, 40)

    first_pair("far")
    ring_1.far()
    first_pair("right")
    ring_1.near_right()
    first_pair("left")
    ring_1.near_left()
    out_chunk("right")
    ring_c.near_right()
    out_chunk("left")
    ring_c.near_left()
    state.step2()
    copies.sent(pair_m)
    copies.sent(pair_q)
    first_pair("own")
    in_v.wait()
    flip(wslot.at[1], wvn)
    ring_c.combine()
    in_k.wait()
    flip(wslot.at[0], wkn)
    state.step3()
    ring_1.combine()

    state.done()

    def key_value_grad(h):
        high, low = parts(bfin[head(h), :])
        kt, vt = k[head(h), :], v[block(h), :]
        one = dot(high, vt) + dot(low, vt)
        one = jnp.where(kt.astype(f32) > 0, one, 0.0).astype(bf16)
        two = (dot_n(high, kt) + dot_n(low, kt))[0:HD, :].astype(bf16)
        rhs2[head(h), 0:T] = one
        send[head(h), :] = one.astype(f32)
        at = pl.ds(W + h * HD, HD)
        rhs2[at, 0:T] = two
        send[at, :] = two.astype(f32)

    each(HEADS, key_value_grad)
    pair = copies.start(send, recv, partner)

    def in_chunk(which):
        rows = y_rows(which)
        dp[pl.ds(order[which] * W, W), :] = (
            dot(wqn[rows, :], rhs1[W:2 * W, 0:T]) + dot(wkn[rows, :], rhs2[0:W, 0:T])
            + dot(wvn[rows, :], rhs2[W:2 * W, 0:T]))

    ring_d = Ring(copies, down, up, y_slot(dp), dbox, W // 2)
    in_chunk("far")
    ring_d.far()
    in_chunk("right")
    ring_d.near_right()
    pair.wait_recv()
    take_pair(rhs2, 0)
    take_pair(rhs2, W)
    ring_1.sent(("a0", "a1"))
    second_pair("far")
    ring_2.far()
    in_chunk("left")
    ring_d.near_left()
    second_pair("own")
    out_chunk("own")
    in_chunk("own")

    ring_1.sent(("d0", "d1", "c0", "c1"))
    second_pair("right")
    ring_2.near_right()
    second_pair("left")
    ring_2.near_left()

    def add_up(dst, box, rows, tile):
        def step(i):
            r = pl.ds(pl.multiple_of(i * tile, 8), tile)
            dst[r, :] = dst[r, :] + (box[1, r, :] + box[2, r, :])

        loop(rows // tile, step)

    ring_1.arrived()
    add_up(own1, box1, CH, 96)
    ring_p.far()
    ring_p.near_right()
    ring_p.near_left()

    def y_sum(buf, box, dst, out, sem):
        def step(i):
            at = pl.ds(pl.multiple_of(3 * W + i * HD, 16), HD)
            rb = pl.ds(pl.multiple_of(i * HD, 16), HD)
            dst[rb, :] = (buf[at, :] + (box[1, rb, :] + box[2, rb, :])).astype(bf16)

        loop(HEADS, step)
        return local(dst, out, sem)

    ring_c.arrived()
    out_c = y_sum(cp, cbox, q, at_o, out_sem.at[0])

    ring_2.combine()
    ring_d.combine()
    ring_p.combine()

    def final(src, box, out, sem):
        rows = pl.ds(pl.multiple_of(sa * RP, 8), RP)
        src[rows, :] = src[rows, :] + (box[1] + box[2])
        return local(src.at[rows, :], out, sem)

    ring_p.arrived()
    out_1 = final(own1, pbox1, g1_o, out_sem.at[1])

    ring_2.arrived()
    add_up(own2, box2, CH, 96)
    ring_r.far()
    ring_r.near_right()
    ring_r.near_left()
    ring_r.combine()
    ring_r.arrived()
    out_2 = final(own2, pbox2, g2_o, out_sem.at[2])

    ring_d.arrived()
    out_d = y_sum(dp, dbox, gm, gt_o, out_sem.at[3])
    copies.finish()
    for copy in (out_c, out_1, out_2, out_d):
        copy.wait()


def finish(factor, at, gt, g1, g2, at_o, gt_o, gq_o, gk_o, gv_o, gw_o):
    at_o[...] = at[...]
    gt_o[...] = gt[...]
    one, two = g1[0:ROWS, :] * factor, g2[0:ROWS, :] * factor
    gw_o[...] = one[:, 0:W]
    gq_o[...] = one[:, W:2 * W]
    gk_o[...] = two[:, 0:W]
    gv_o[...] = two[:, W:2 * W]


def body(tokens, w_query, w_key, w_value, w_out, grad_out):
    shapes = [
        ((D, T), bf16), ((D, T), bf16), ((2, W, D), bf16),
        ((D, W), bf16), ((D, W), bf16), ((D, W), bf16), ((D, W), bf16),
        ((GR, 2 * T), bf16), ((GR, 2 * T), bf16),
        ((W, T), bf16), ((W, T), bf16), ((HEADS * HP, T), bf16), ((W, T), bf16),
        ((HEADS * HP, T), bf16), ((HEADS * HP, T), bf16),
        ((GC, 2 * T), bf16), ((GC, 2 * T), bf16), ((2 * W, T), f32), ((2 * W, T), f32),
        ((3 * CH, GC), f32), ((CH, GC), f32), ((CH, GC), f32),
        ((3, CH, GC), f32), ((3, CH, GC), f32), ((3, RP, GC), f32), ((3, RP, GC), f32),
        ((2 * GR, T), f32), ((2 * GR, T), f32), ((3, W, T), f32), ((3, W, T), f32),
    ]
    for _ in range(2):
        shapes += [((SR, HP), f32), ((SR // 2, HP), f32), ((NB - 1, PR, HP), f32), ((SR, HP), f32)]
    scratch = [pltpu.VMEM(*shape) for shape in shapes]
    scratch += [
        pltpu.SemaphoreType.DMA((6,)), pltpu.SemaphoreType.DMA((4,)),
        pltpu.SemaphoreType.DMA((112,)), pltpu.SemaphoreType.DMA((112,)),
    ]
    spaces = [pl.BlockSpec(memory_space=pl.ANY)] * 6
    at, gt, g1, g2 = pl.pallas_call(
        kernel,
        out_shape=(
            jax.ShapeDtypeStruct((W, T), bf16), jax.ShapeDtypeStruct((W, T), bf16),
            jax.ShapeDtypeStruct((RP, GC), f32), jax.ShapeDtypeStruct((RP, GC), f32),
        ),
        in_specs=spaces,
        out_specs=spaces[:4],
        scratch_shapes=scratch,
        compiler_params=pltpu.CompilerParams(
            collective_id=0, has_side_effects=True, vmem_limit_bytes=64 * 1024 * 1024 - 65536),
        cost_estimate=pl.CostEstimate(flops=16 * 10**9, bytes_accessed=16 * 10**6, transcendentals=0),
        name="fused_attention",
    )(tokens.T, w_query.T, w_key.T, w_value.T, w_out, grad_out.T)
    factor = 1.0 / math.sqrt(T * lax.axis_size("seq"))
    grad = jax.ShapeDtypeStruct((ROWS, W), f32)
    vmem = pl.BlockSpec(memory_space=pltpu.VMEM)
    at, gt, gq, gk, gv, gw = pl.pallas_call(
        functools.partial(finish, factor),
        out_shape=(
            jax.ShapeDtypeStruct((W, T), bf16), jax.ShapeDtypeStruct((W, T), bf16),
            grad, grad, grad, grad,
        ),
        in_specs=[vmem] * 4,
        out_specs=[vmem] * 6,
        name="final_arrays",
    )(at, gt, g1, g2)
    return (at.T, gt.T, gq, gk, gv, gw.T)


def solution(mesh):
    in_specs = (
        P("seq", None),
        P(None, "head"),
        P(None, "head"),
        P(None, "head"),
        P("head", None),
        P("seq", None),
    )
    out_specs = (
        P("seq", "head"),
        P("seq", "head"),
        P("seq", "head"),
        P("seq", "head"),
        P("seq", "head"),
        P("head", "seq"),
    )
    return jax.shard_map(body, mesh=mesh, in_specs=in_specs, out_specs=out_specs, check_vma=False)
```

```python
import functools
import math

import jax
import jax.numpy as jnp
from jax import lax
from jax.experimental import pallas as pl
from jax.experimental.pallas import tpu as pltpu
from jax.sharding import PartitionSpec as P

f32 = jnp.float32
bf16 = jnp.bfloat16
MESH = pl.DeviceIdType.MESH

D = 2240
W = 560
HEADS = 5
HP = 128
T = 384
HD = 112
ROWS = 70
RP = 72
NB = 16
GR = NB * RP
GC = 1152
WP = 640
CH = 4 * RP
PR = 24
SR = 2 * NB * PR
EPS = 1e-15


def dot(a, b):
    return lax.dot_general(a, b, (((1,), (0,)), ((), ())), preferred_element_type=f32)


def dot_t(a, b):
    return lax.dot_general(a, b, (((1,), (1,)), ((), ())), preferred_element_type=f32)


def dot_n(a, b):
    return lax.dot_general(a, b, (((0,), (0,)), ((), ())), preferred_element_type=f32)


def parts(v):
    high = v.astype(bf16)
    return high, (v - high.astype(f32)).astype(bf16)


def each(count, fn):
    for i in range(count):
        fn(i)


def loop(count, fn):
    def step(i, carry):
        fn(i)
        return carry

    lax.fori_loop(0, count, step, 0)


class Copies:
    def __init__(self, send, recv):
        self.send, self.recv, self.used, self.open = send, recv, 0, []

    def start(self, src, dst, device):
        k = self.used
        self.used += 1
        copy = pltpu.make_async_remote_copy(
            src_ref=src, dst_ref=dst, send_sem=self.send.at[k], recv_sem=self.recv.at[k],
            device_id=device, device_id_type=MESH)
        copy.start()
        self.open.append(copy)
        return copy

    def sent(self, copy):
        copy.wait_send()
        self.open = [other for other in self.open if other is not copy]

    def finish(self):
        for copy in self.open:
            copy.wait_send()
        self.open = []


class Ring:
    def __init__(self, copies, left, right, slot, box, cut):
        self.copies, self.left, self.right, self.slot = copies, left, right, slot
        self.box, self.cut = box, cut
        self.rows = box.shape[1]

    def land(self, kind, half):
        if half == 0:
            return self.box.at[kind, pl.ds(0, self.cut), :]
        return self.box.at[kind, pl.ds(self.cut, self.rows - self.cut), :]

    def far(self):
        self.a0 = self.copies.start(self.slot("far", 0), self.land(0, 0), self.right)
        self.a1 = self.copies.start(self.slot("far", 1), self.land(0, 1), self.left)

    def near_right(self):
        self.d1 = self.copies.start(self.slot("right", 1), self.land(1, 1), self.right)

    def near_left(self):
        self.d0 = self.copies.start(self.slot("left", 0), self.land(1, 0), self.left)

    def combine(self):
        self.a0.wait_recv()
        ref = self.slot("right", 0)
        ref[...] = ref[...] + self.land(0, 0)[...]
        self.c0 = self.copies.start(ref, self.land(2, 0), self.right)
        self.a1.wait_recv()
        ref = self.slot("left", 1)
        ref[...] = ref[...] + self.land(0, 1)[...]
        self.c1 = self.copies.start(ref, self.land(2, 1), self.left)

    def arrived(self):
        for copy in (self.d0, self.d1, self.c0, self.c1):
            copy.wait_recv()

    def sent(self, names):
        for name in names:
            self.copies.sent(getattr(self, name))


def kernel(tok_h, wq_h, wk_h, wv_h, wo_h, go_h,
           at_o, gt_o, g1_o, g2_o, g3_o,
           tok, go, wslot, wot, wqn, wkn, wvn, tokt, got,
           q, v, gm, kx, rhs1, rhs2, send, recv,
           gbuf, tbuf, own1, own2, own3, box1, box2, box3, pbox1, pbox2, pbox3,
           cp, dp, cbox, dbox,
           sta, a0, a1, afin, stb, b0, b1, bfin,
           in_sem, out_sem, ssem, rsem):
    s = lax.axis_index("seq")
    y = lax.axis_index("head")
    c = s % 2
    chip = s // 2
    x = chip // 4
    z = chip % 4
    fa = x * (1 - c) + z * c
    sa = z * (1 - c) + x * c

    def first(i):
        return {"seq": ((i * (1 - c) + sa * c) * 4 + sa * (1 - c) + i * c) * 2 + c, "head": y}

    def second(i):
        return {"seq": ((fa * (1 - c) + i * c) * 4 + i * (1 - c) + fa * c) * 2 + c, "head": y}

    def along_y(i):
        return {"seq": s, "head": i}

    def chip_at(dx, dz):
        return {"seq": ((x + dx) % 4 * 4 + (z + dz) % 4) * 2 + c, "head": y}

    others = sorted([(dx, dz) for dx in range(4) for dz in range(4) if dx or dz],
                    key=lambda place: -sum(min(d, 4 - d) for d in place))
    partner = {"seq": s + 1 - 2 * c, "head": y}

    def local(src, dst, sem):
        copy = pltpu.make_async_copy(src, dst, sem)
        copy.start()
        return copy

    in_tok = local(tok_h, tok, in_sem.at[0])
    in_k = local(wk_h, wslot.at[0], in_sem.at[1])
    in_v = local(wv_h, wslot.at[1], in_sem.at[2])
    in_go = local(go_h, go, in_sem.at[3])

    barrier = pltpu.get_barrier_semaphore()
    peers = [partner, along_y((y + 1) % 4), along_y((y + 3) % 4)]
    peers += [chip_at(*place) for place in others]
    for peer in peers:
        pl.semaphore_signal(barrier, inc=1, device_id=peer, device_id_type=MESH)

    copies = Copies(ssem, rsem)

    def head(h):
        return pl.ds(h * HD, HD)

    def block(h):
        return pl.ds(h * HP, HP)

    def sum_row(row):
        keep = lax.broadcasted_iota(jnp.int32, (HP - HD, T), 0) == 0
        return jnp.where(keep, row, 0.0)

    def state_part(st, left, rights):
        def one(h):
            total = None
            for right in rights:
                value = dot_t(left[head(h), :], right[block(h), :])
                total = value if total is None else total + value
            st[head(h), :] = total

        each(HEADS, one)
        st[W:SR, :] = jnp.zeros((SR - W, HP), f32)

    half = SR // 2
    mine = pl.multiple_of(c * half, 8)
    other = pl.multiple_of((1 - c) * half, 8)

    def piece(dx, dz):
        place = (x + dx) % 4 * 4 + (z + dz) % 4
        return pl.ds(pl.multiple_of(c * half + place * PR, 8), PR)

    class State:
        def __init__(self, st, r0, r1, fin):
            self.st, self.r0, self.r1, self.fin = st, r0, r1, fin

        def step0(self):
            self.c = copies.start(self.st.at[pl.ds(other, half), :], self.r0, partner)

        def step1(self):
            self.c.wait_recv()
            rows = pl.ds(mine, half)
            self.st[rows, :] = self.st[rows, :] + self.r0[...]
            self.cs = [copies.start(self.st.at[piece(*place), :], self.r1.at[i], chip_at(*place))
                       for i, place in enumerate(others)]

        def step2(self):
            for copy in self.cs:
                copy.wait_recv()
            rows = piece(0, 0)
            total = self.st[rows, :]
            for i in range(0, NB - 1, 3):
                total = total + (self.r1[i] + self.r1[i + 1] + self.r1[i + 2])
            self.fin[rows, :] = total
            self.cs = [copies.start(self.fin.at[rows, :], self.fin.at[rows, :], chip_at(*place))
                       for place in others]

        def step3(self):
            for copy in self.cs:
                copy.wait_recv()
            rows = pl.ds(mine, half)
            self.c = copies.start(self.fin.at[rows, :], self.fin.at[rows, :], partner)

        def done(self):
            self.c.wait_recv()

    def gather_rows(src, base, which):
        for b in range(NB):
            lo = 2 * ROWS * b
            w0 = lo // 16 * 16
            w1 = -(-(lo + 2 * ROWS) // 16) * 16
            i = lax.broadcasted_iota(jnp.int32, (RP, w1 - w0), 0)
            j = lax.broadcasted_iota(jnp.int32, (RP, w1 - w0), 1)
            pick = jnp.logical_and(j == i + (lo - w0) + ROWS * which, i < ROWS)
            place = b * (1 - which) + (b % 4 * 4 + b // 4) * which
            cp[pl.ds(pl.multiple_of(base + place * RP, 8), RP), :] = dot(
                pick.astype(f32).astype(bf16), src[w0:w1, :])

    def own_rows(src, dst, base):
        gather_rows(src, base, c)

        def cast(i):
            r = pl.multiple_of(i * 288, 16)
            dst[pl.ds(r, 288), 0:T] = cp[pl.ds(pl.multiple_of(base + r, 8), 288), :].astype(bf16)

        loop(GR // 288, cast)

    def send_rows(src, base):
        gather_rows(src, base, 1 - c)
        place = pl.ds(base, GR)
        return copies.start(cp.at[place, :], dp.at[place, :], partner)

    def flip(src, dst):
        for start in range(0, D, 256):
            n = min(256, D - start)
            dst[start:start + n, :] = src[:, start:start + n].T

    def cast_rows(dst, base):
        def cast(i):
            r = pl.multiple_of(i * 288, 16)
            dst[pl.ds(r, 288), T:2 * T] = dp[pl.ds(pl.multiple_of(base + r, 8), 288), :].astype(bf16)

        loop(GR // 288, cast)

    def take_pair(dst, base, source):
        def cast(i):
            r = pl.multiple_of(i * HD, 16)
            dst[pl.ds(base + r, HD), T:2 * T] = recv[pl.ds(source + r, HD), :].astype(bf16)

        loop(W // HD, cast)

    first_half, second_half = pl.ds(0, W), pl.ds(W, W)
    order = {"far": 0, "right": 1, "left": 2, "own": 3}

    ring_f = {"far": (fa + 2) % 4, "right": (fa + 1) % 4, "left": (fa + 3) % 4, "own": fa}
    fr, fl = first((fa + 1) % 4), first((fa + 3) % 4)
    sr, sl = second((sa + 1) % 4), second((sa + 3) % 4)

    def g_slot(buf):
        def slot(which, h):
            return buf.at[pl.ds(order[which] * CH + h * 144, 144), :]

        return slot

    def p_slot(buf):
        far = {"far": (sa + 2) % 4, "right": (sa + 1) % 4, "left": (sa + 3) % 4}

        def slot(which, h):
            base = far[which] * RP
            if h == 0:
                return buf.at[pl.ds(pl.multiple_of(base, 8), 40), :]
            return buf.at[pl.ds(pl.multiple_of(base + 40, 8), 32), :]

        return slot

    ring_1 = Ring(copies, fl, fr, g_slot(gbuf), box1, 144)
    ring_2 = Ring(copies, fl, fr, g_slot(tbuf), box2, 144)
    ring_3 = Ring(copies, fl, fr, g_slot(tbuf), box3, 144)
    ring_1p = Ring(copies, sl, sr, p_slot(own1), pbox1, 40)
    ring_2p = Ring(copies, sl, sr, p_slot(own2), pbox2, 40)
    ring_3p = Ring(copies, sl, sr, p_slot(own3), pbox3, 40)

    def chunk_of(which):
        rows = pl.ds(pl.multiple_of(ring_f[which] * CH, 16), CH)
        base = 0 if which == "own" else order[which] * CH
        return rows, pl.ds(base, CH)

    def first_pair(which):
        rows, to = chunk_of(which)
        dst = own1 if which == "own" else gbuf
        lo, lt = got[rows, :], tokt[rows, :]
        dst[to, 0:512] = dot_t(lo, rhs1[0:512, :])
        shared = rhs1[512:640, :]
        is_out = lax.broadcasted_iota(jnp.int32, (CH, 128), 1) < W - 512
        dst[to, 512:640] = jnp.where(is_out, dot_t(lo, shared), dot_t(lt, shared))
        dst[to, 640:GC] = dot_t(lt, rhs1[640:GC, :])

    def key_chunk(which):
        rows, to = chunk_of(which)
        dst = own2 if which == "own" else tbuf
        dst[to, :] = dot_t(tokt[rows, :], rhs2[...])

    def moment_chunk(which):
        rows, to = chunk_of(which)
        dst = own3 if which == "own" else tbuf
        dst[to, :] = dot_t(tokt[rows, :], kx[...])

    def add_up(dst, box, rows, tile):
        def step(i):
            r = pl.ds(pl.multiple_of(i * tile, 8), tile)
            dst[r, :] = dst[r, :] + (box[1, r, :] + box[2, r, :])

        loop(rows // tile, step)

    in_tok.wait()
    in_k.wait()
    value = jnp.maximum(dot(wslot[0], tok[...]), 0.0).astype(bf16)
    k = kx.at[pl.ds(0, W), pl.ds(0, T)]
    k[...] = value
    send[first_half, :] = value.astype(f32)
    in_q = local(wq_h, wslot.at[0], in_sem.at[4])
    pl.semaphore_wait(barrier, len(peers))
    pair_k = copies.start(send.at[first_half, :], recv.at[first_half, :], partner)
    in_v.wait()
    value = dot(wslot[1], tok[...]).astype(bf16)
    for h in range(HEADS):
        v[HP * h:HP * h + HD, :] = value[HD * h:HD * h + HD, :]
        v[HP * h + HD:HP * h + HP, :] = sum_row(jnp.ones((1, T), f32)).astype(bf16)
    in_o = local(wo_h, wslot.at[1], in_sem.at[5])
    state_part(sta, k, [v])
    state = State(sta, a0, a1, afin)
    state.step0()
    send_tok = send_rows(tok, 0)

    in_q.wait()
    q[...] = jnp.maximum(dot(wslot[0], tok[...]), 0.0).astype(bf16)
    state.step1()
    own_rows(tok, tokt, GR)
    kx[W:WP, :] = jnp.zeros((WP - W, 2 * T), bf16)
    rhs1[2 * W:GC, :] = jnp.zeros((GC - 2 * W, 2 * T), bf16)
    rhs2[W:WP, :] = jnp.zeros((WP - W, 2 * T), bf16)
    pair_k.wait_recv()
    take_pair(kx, 0, 0)
    send_tok.wait_recv()
    cast_rows(tokt, 0)
    moment_chunk("far")
    ring_3.far()
    moment_chunk("right")
    moment_chunk("left")
    in_o.wait()
    in_go.wait()
    gm[...] = dot(wslot[1], go[...]).astype(bf16)
    state.step2()
    ring_3.near_right()
    ring_3.near_left()
    ring_3.combine()
    send_go = send_rows(go, GR)
    flip(wslot.at[1], wot)
    in_v = local(wv_h, wslot.at[1], in_sem.at[2])
    copies.sent(send_tok)
    own_rows(go, got, 0)
    moment_chunk("own")
    state.step3()
    send_go.wait_recv()
    cast_rows(got, GR)
    flip(wslot.at[0], wqn)
    in_k = local(wk_h, wslot.at[0], in_sem.at[1])
    copies.sent(pair_k)
    state.done()

    dv, ngh, ngl = (tok.at[pl.ds(WP * i, WP), :] for i in range(3))

    def attend(h):
        high, low = parts(afin[head(h), :])
        qt = q[head(h), :]
        both = dot_n(high, qt) + dot_n(low, qt)
        rec = 1.0 / (both[HD:HD + 1, :] + EPS)
        att = both[0:HD, :] * rec
        rhs1[head(h), 0:T] = att.astype(bf16)
        send[head(h), :] = att.astype(bf16).astype(f32)
        g = gm[head(h), :].astype(f32)
        grad = -jnp.sum(g * att, axis=0, keepdims=True) * rec
        high, low = parts(g * rec)
        at = pl.ds(h * HP, HD)
        ngh[at, :] = high
        ngl[at, :] = low
        high, low = parts(sum_row(grad))
        at = pl.ds(h * HP + HD, HP - HD)
        ngh[at, :] = high
        ngl[at, :] = low

    each(HEADS, attend)
    pair_m = copies.start(send.at[first_half, :], recv.at[first_half, :], partner)

    ring_y = {"far": (y + 2) % 4, "right": (y + 1) % 4, "left": (y + 3) % 4, "own": y}
    copies.sent(send_go)

    def y_rows(which):
        return pl.ds(pl.multiple_of(ring_y[which] * W, 16), W)

    def out_chunk(which):
        cp[pl.ds(order[which] * W, W), :] = dot(wot[y_rows(which), :], rhs1[0:W, 0:T])

    def y_slot(buf):
        def slot(which, h):
            return buf.at[pl.ds(order[which] * W + h * (W // 2), W // 2), :]

        return slot

    up, down = along_y((y + 1) % 4), along_y((y + 3) % 4)
    ring_c = Ring(copies, down, up, y_slot(cp), cbox, W // 2)
    out_chunk("far")
    ring_c.far()

    state_part(stb, q, [ngh, ngl])
    state = State(stb, b0, b1, bfin)
    state.step0()

    def query_grad(h):
        high, low = parts(afin[head(h), :])
        ng = ngh[block(h), :]
        value = dot(high, ng) + dot(low, ng) + dot(high, ngl[block(h), :])
        value = jnp.where(q[head(h), :].astype(f32) > 0, value, 0.0).astype(bf16)
        at = pl.ds(W + h * HD, HD)
        rhs1[at, 0:T] = value
        send[at, :] = value.astype(f32)

    each(HEADS, query_grad)
    pair_q = copies.start(send.at[second_half, :], recv.at[second_half, :], partner)
    state.step1()
    ring_3.arrived()
    add_up(own3, box3, CH, 96)
    ring_3p.far()
    ring_3p.near_right()
    ring_3p.near_left()
    pair_m.wait_recv()
    take_pair(rhs1, 0, 0)
    pair_q.wait_recv()
    take_pair(rhs1, W, W)
    first_pair("far")
    ring_1.far()
    out_chunk("right")
    ring_c.near_right()
    out_chunk("left")
    ring_c.near_left()
    first_pair("right")
    first_pair("left")
    state.step2()
    ring_1.near_right()
    ring_1.near_left()
    copies.sent(pair_m)
    copies.sent(pair_q)
    ring_3p.combine()
    in_v.wait()
    flip(wslot.at[1], wvn)
    in_k.wait()
    flip(wslot.at[0], wkn)
    ring_c.combine()
    first_pair("own")
    state.step3()
    ring_1.combine()

    state.done()

    def key_value_grad(h):
        high, low = parts(bfin[head(h), :])
        kt, vt = k[head(h), :], v[block(h), :]
        one = dot(high, vt) + dot(low, vt)
        one = jnp.where(kt.astype(f32) > 0, one, 0.0).astype(bf16)
        rhs2[head(h), 0:T] = one
        send[head(h), :] = one.astype(f32)
        dv[head(h), :] = (dot_n(high, kt) + dot_n(low, kt))[0:HD, :].astype(bf16)

    each(HEADS, key_value_grad)
    pair = copies.start(send.at[first_half, :], recv.at[first_half, :], partner)

    def in_chunk(which):
        rows = y_rows(which)
        dp[pl.ds(order[which] * W, W), :] = (
            dot(wqn[rows, :], rhs1[W:2 * W, 0:T]) + dot(wkn[rows, :], rhs2[0:W, 0:T])
            + dot(wvn[rows, :], dv[0:W, :]))

    ring_d = Ring(copies, down, up, y_slot(dp), dbox, W // 2)
    in_chunk("far")
    ring_d.far()
    pair.wait_recv()
    take_pair(rhs2, 0, 0)
    ring_3.sent(("a0", "a1", "d0", "d1", "c0", "c1"))
    key_chunk("far")
    ring_2.far()
    in_chunk("right")
    ring_d.near_right()
    in_chunk("left")
    ring_d.near_left()
    key_chunk("right")
    ring_2.near_right()
    key_chunk("left")
    ring_2.near_left()
    key_chunk("own")
    out_chunk("own")
    in_chunk("own")

    def final(src, box, out, sem):
        rows = pl.ds(pl.multiple_of(sa * RP, 8), RP)
        src[rows, :] = src[rows, :] + (box[1] + box[2])
        return local(src.at[rows, :], out, sem)

    ring_3p.arrived()
    rows = pl.ds(pl.multiple_of(sa * RP, 8), RP)
    moment = own3[rows, :] + (pbox3[1] + pbox3[2])
    for h in range(HEADS):
        high, low = parts(moment[:, HD * h:HD * h + HD])
        state_high, state_low = parts(bfin[head(h), 0:HD])
        pbox3[0, :, HD * h:HD * h + HD] = (
            dot(high, state_high) + dot(high, state_low) + dot(low, state_high))
    out_3 = local(pbox3.at[0], g3_o, out_sem.at[4])

    ring_1.arrived()
    add_up(own1, box1, CH, 96)
    ring_1p.far()
    ring_1p.near_right()
    ring_1p.near_left()

    def y_sum(buf, box, dst, out, sem):
        def step(i):
            at = pl.ds(pl.multiple_of(3 * W + i * HD, 16), HD)
            rb = pl.ds(pl.multiple_of(i * HD, 16), HD)
            dst[rb, :] = (buf[at, :] + (box[1, rb, :] + box[2, rb, :])).astype(bf16)

        loop(HEADS, step)
        return local(dst, out, sem)

    ring_c.arrived()
    out_c = y_sum(cp, cbox, q, at_o, out_sem.at[0])

    ring_2.combine()
    ring_d.combine()
    ring_1p.combine()
    ring_2.arrived()
    add_up(own2, box2, CH, 96)
    ring_2p.far()
    ring_2p.near_right()
    ring_2p.near_left()
    ring_1p.arrived()
    out_1 = final(own1, pbox1, g1_o, out_sem.at[1])
    ring_2p.combine()
    ring_2p.arrived()
    out_2 = final(own2, pbox2, g2_o, out_sem.at[2])

    ring_d.arrived()
    out_d = y_sum(dp, dbox, gm, gt_o, out_sem.at[3])
    copies.finish()
    for copy in (out_c, out_1, out_2, out_3, out_d):
        copy.wait()


def finish(factor, at, gt, g1, g2, g3, at_o, gt_o, gq_o, gk_o, gv_o, gw_o):
    at_o[...] = at[...]
    gt_o[...] = gt[...]
    one = g1[0:ROWS, :] * factor
    gw_o[...] = one[:, 0:W]
    gq_o[...] = one[:, W:2 * W]
    gk_o[...] = g2[0:ROWS, 0:W] * factor
    gv_o[...] = g3[0:ROWS, 0:W] * factor


def body(tokens, w_query, w_key, w_value, w_out, grad_out):
    shapes = [
        ((D, T), bf16), ((D, T), bf16), ((2, W, D), bf16),
        ((D, W), bf16), ((D, W), bf16), ((D, W), bf16), ((D, W), bf16),
        ((GR, 2 * T), bf16), ((GR, 2 * T), bf16),
        ((W, T), bf16), ((HEADS * HP, T), bf16), ((W, T), bf16), ((WP, 2 * T), bf16),
        ((GC, 2 * T), bf16), ((WP, 2 * T), bf16), ((2 * W, T), f32), ((2 * W, T), f32),
        ((3 * CH, GC), f32), ((3 * CH, WP), f32), ((CH, GC), f32), ((CH, WP), f32), ((CH, WP), f32),
        ((3, CH, GC), f32), ((3, CH, WP), f32), ((3, CH, WP), f32),
        ((3, RP, GC), f32), ((3, RP, WP), f32), ((3, RP, WP), f32),
        ((2 * GR, T), f32), ((2 * GR, T), f32), ((3, W, T), f32), ((3, W, T), f32),
    ]
    for _ in range(2):
        shapes += [((SR, HP), f32), ((SR // 2, HP), f32), ((NB - 1, PR, HP), f32), ((SR, HP), f32)]
    scratch = [pltpu.VMEM(*shape) for shape in shapes]
    scratch += [
        pltpu.SemaphoreType.DMA((6,)), pltpu.SemaphoreType.DMA((5,)),
        pltpu.SemaphoreType.DMA((120,)), pltpu.SemaphoreType.DMA((120,)),
    ]
    spaces = [pl.BlockSpec(memory_space=pl.ANY)] * 6
    at, gt, g1, g2, g3 = pl.pallas_call(
        kernel,
        out_shape=(
            jax.ShapeDtypeStruct((W, T), bf16), jax.ShapeDtypeStruct((W, T), bf16),
            jax.ShapeDtypeStruct((RP, GC), f32), jax.ShapeDtypeStruct((RP, WP), f32),
            jax.ShapeDtypeStruct((RP, WP), f32),
        ),
        in_specs=spaces,
        out_specs=spaces[:5],
        scratch_shapes=scratch,
        compiler_params=pltpu.CompilerParams(
            collective_id=0, has_side_effects=True, vmem_limit_bytes=64 * 1024 * 1024 - 65536),
        cost_estimate=pl.CostEstimate(flops=16 * 10**9, bytes_accessed=16 * 10**6, transcendentals=0),
        name="fused_attention",
    )(tokens.T, w_query.T, w_key.T, w_value.T, w_out, grad_out.T)
    factor = 1.0 / math.sqrt(T * lax.axis_size("seq"))
    grad = jax.ShapeDtypeStruct((ROWS, W), f32)
    vmem = pl.BlockSpec(memory_space=pltpu.VMEM)
    at, gt, gq, gk, gv, gw = pl.pallas_call(
        functools.partial(finish, factor),
        out_shape=(
            jax.ShapeDtypeStruct((W, T), bf16), jax.ShapeDtypeStruct((W, T), bf16),
            grad, grad, grad, grad,
        ),
        in_specs=[vmem] * 5,
        out_specs=[vmem] * 6,
        name="final_arrays",
    )(at, gt, g1, g2, g3)
    return (at.T, gt.T, gq, gk, gv, gw.T)


def solution(mesh):
    in_specs = (
        P("seq", None),
        P(None, "head"),
        P(None, "head"),
        P(None, "head"),
        P("head", None),
        P("seq", None),
    )
    out_specs = (
        P("seq", "head"),
        P("seq", "head"),
        P("seq", "head"),
        P("seq", "head"),
        P("seq", "head"),
        P("head", "seq"),
    )
    return jax.shard_map(body, mesh=mesh, in_specs=in_specs, out_specs=out_specs, check_vma=False)
```

```python
import functools
import math

import jax
import jax.numpy as jnp
from jax import lax
from jax.experimental import pallas as pl
from jax.experimental.pallas import tpu as pltpu
from jax.sharding import PartitionSpec as P

f32 = jnp.float32
bf16 = jnp.bfloat16
MESH = pl.DeviceIdType.MESH

D = 2240
W = 560
HEADS = 5
HP = 128
T = 384
HD = 112
ROWS = 70
RP = 72
NB = 16
GR = NB * RP
GC = 1152
WP = 640
CH = 4 * RP
PR = 24
SR = 2 * NB * PR
EPS = 1e-15


def dot(a, b):
    return lax.dot_general(a, b, (((1,), (0,)), ((), ())), preferred_element_type=f32)


def dot_t(a, b):
    return lax.dot_general(a, b, (((1,), (1,)), ((), ())), preferred_element_type=f32)


def dot_n(a, b):
    return lax.dot_general(a, b, (((0,), (0,)), ((), ())), preferred_element_type=f32)


def parts(v):
    high = v.astype(bf16)
    return high, (v - high.astype(f32)).astype(bf16)


def each(count, fn):
    for i in range(count):
        fn(i)


def loop(count, fn):
    def step(i, carry):
        fn(i)
        return carry

    lax.fori_loop(0, count, step, 0)


class Copies:
    def __init__(self, send, recv):
        self.send, self.recv, self.used, self.open = send, recv, 0, []

    def start(self, src, dst, device):
        k = self.used
        self.used += 1
        copy = pltpu.make_async_remote_copy(
            src_ref=src, dst_ref=dst, send_sem=self.send.at[k], recv_sem=self.recv.at[k],
            device_id=device, device_id_type=MESH)
        copy.start()
        self.open.append(copy)
        return copy

    def sent(self, copy):
        copy.wait_send()
        self.open = [other for other in self.open if other is not copy]

    def finish(self):
        for copy in self.open:
            copy.wait_send()
        self.open = []


class Ring:
    def __init__(self, copies, left, right, slot, box, cut):
        self.copies, self.left, self.right, self.slot = copies, left, right, slot
        self.box, self.cut = box, cut
        self.rows = box.shape[1]

    def land(self, kind, half):
        if half == 0:
            return self.box.at[kind, pl.ds(0, self.cut), :]
        return self.box.at[kind, pl.ds(self.cut, self.rows - self.cut), :]

    def far(self):
        self.a0 = self.copies.start(self.slot("far", 0), self.land(0, 0), self.right)
        self.a1 = self.copies.start(self.slot("far", 1), self.land(0, 1), self.left)

    def near_right(self):
        self.d1 = self.copies.start(self.slot("right", 1), self.land(1, 1), self.right)

    def near_left(self):
        self.d0 = self.copies.start(self.slot("left", 0), self.land(1, 0), self.left)

    def combine(self):
        self.a0.wait_recv()
        ref = self.slot("right", 0)
        ref[...] = ref[...] + self.land(0, 0)[...]
        self.c0 = self.copies.start(ref, self.land(2, 0), self.right)
        self.a1.wait_recv()
        ref = self.slot("left", 1)
        ref[...] = ref[...] + self.land(0, 1)[...]
        self.c1 = self.copies.start(ref, self.land(2, 1), self.left)

    def arrived(self):
        for copy in (self.d0, self.d1, self.c0, self.c1):
            copy.wait_recv()

    def sent(self, names):
        for name in names:
            self.copies.sent(getattr(self, name))


def kernel(tok_h, wq_h, wk_h, wv_h, wo_h, go_h,
           at_o, gt_o, g1_o, g2_o, g3_o,
           tok, go, wslot, wot, wqn, wkn, wvn, tokt, got,
           q, v, gm, kx, rhs1, rhs2, send, recv,
           gbuf, tbuf, own1, own2, own3, box1, box2, box3, pbox1, pbox2, pbox3,
           cp, dp, cbox, dbox,
           sta, a0, a1, afin, stb, b0, b1, bfin,
           in_sem, out_sem, ssem, rsem):
    s = lax.axis_index("seq")
    y = lax.axis_index("head")
    c = s % 2
    chip = s // 2
    x = chip // 4
    z = chip % 4
    fa = x * (1 - c) + z * c
    sa = z * (1 - c) + x * c

    def first(i):
        return {"seq": ((i * (1 - c) + sa * c) * 4 + sa * (1 - c) + i * c) * 2 + c, "head": y}

    def second(i):
        return {"seq": ((fa * (1 - c) + i * c) * 4 + i * (1 - c) + fa * c) * 2 + c, "head": y}

    def along_y(i):
        return {"seq": s, "head": i}

    def chip_at(dx, dz):
        return {"seq": ((x + dx) % 4 * 4 + (z + dz) % 4) * 2 + c, "head": y}

    others = sorted([(dx, dz) for dx in range(4) for dz in range(4) if dx or dz],
                    key=lambda place: -sum(min(d, 4 - d) for d in place))
    partner = {"seq": s + 1 - 2 * c, "head": y}

    def local(src, dst, sem):
        copy = pltpu.make_async_copy(src, dst, sem)
        copy.start()
        return copy

    in_tok = local(tok_h, tok, in_sem.at[0])
    in_k = local(wk_h, wslot.at[0], in_sem.at[1])
    in_v = local(wv_h, wslot.at[1], in_sem.at[2])
    in_go = local(go_h, go, in_sem.at[3])

    barrier = pltpu.get_barrier_semaphore()
    peers = [partner, along_y((y + 1) % 4), along_y((y + 3) % 4)]
    peers += [chip_at(*place) for place in others]
    for peer in peers:
        pl.semaphore_signal(barrier, inc=1, device_id=peer, device_id_type=MESH)

    copies = Copies(ssem, rsem)

    def head(h):
        return pl.ds(h * HD, HD)

    def block(h):
        return pl.ds(h * HP, HP)

    def sum_row(row):
        keep = lax.broadcasted_iota(jnp.int32, (HP - HD, T), 0) == 0
        return jnp.where(keep, row, 0.0)

    def state_part(st, left, rights):
        def one(h):
            total = None
            for right in rights:
                value = dot_t(left[head(h), :], right[block(h), :])
                total = value if total is None else total + value
            st[head(h), :] = total

        each(HEADS, one)
        st[W:SR, :] = jnp.zeros((SR - W, HP), f32)

    half = SR // 2
    mine = pl.multiple_of(c * half, 8)
    other = pl.multiple_of((1 - c) * half, 8)

    def piece(dx, dz):
        place = (x + dx) % 4 * 4 + (z + dz) % 4
        return pl.ds(pl.multiple_of(c * half + place * PR, 8), PR)

    class State:
        def __init__(self, st, r0, r1, fin):
            self.st, self.r0, self.r1, self.fin = st, r0, r1, fin

        def step0(self):
            self.c = copies.start(self.st.at[pl.ds(other, half), :], self.r0, partner)

        def step1(self):
            self.c.wait_recv()
            rows = pl.ds(mine, half)
            self.st[rows, :] = self.st[rows, :] + self.r0[...]
            self.cs = [copies.start(self.st.at[piece(*place), :], self.r1.at[i], chip_at(*place))
                       for i, place in enumerate(others)]

        def step2(self):
            for copy in self.cs:
                copy.wait_recv()
            rows = piece(0, 0)
            total = self.st[rows, :]
            for i in range(0, NB - 1, 3):
                total = total + (self.r1[i] + self.r1[i + 1] + self.r1[i + 2])
            self.fin[rows, :] = total
            self.cs = [copies.start(self.fin.at[rows, :], self.fin.at[rows, :], chip_at(*place))
                       for place in others]

        def step3(self):
            for copy in self.cs:
                copy.wait_recv()
            rows = pl.ds(mine, half)
            self.c = copies.start(self.fin.at[rows, :], self.fin.at[rows, :], partner)

        def done(self):
            self.c.wait_recv()

    def gather_rows(src, base, which):
        for b in range(NB):
            lo = 2 * ROWS * b
            w0 = lo // 16 * 16
            w1 = -(-(lo + 2 * ROWS) // 16) * 16
            i = lax.broadcasted_iota(jnp.int32, (RP, w1 - w0), 0)
            j = lax.broadcasted_iota(jnp.int32, (RP, w1 - w0), 1)
            pick = jnp.logical_and(j == i + (lo - w0) + ROWS * which, i < ROWS)
            place = b * (1 - which) + (b % 4 * 4 + b // 4) * which
            cp[pl.ds(pl.multiple_of(base + place * RP, 8), RP), :] = dot(
                pick.astype(f32).astype(bf16), src[w0:w1, :])

    def own_rows(src, dst, base):
        gather_rows(src, base, c)

        def cast(i):
            r = pl.multiple_of(i * 288, 16)
            dst[pl.ds(r, 288), 0:T] = cp[pl.ds(pl.multiple_of(base + r, 8), 288), :].astype(bf16)

        loop(GR // 288, cast)

    def send_rows(src, base):
        gather_rows(src, base, 1 - c)
        place = pl.ds(base, GR)
        return copies.start(cp.at[place, :], dp.at[place, :], partner)

    def flip(src, dst):
        for start in range(0, D, 256):
            n = min(256, D - start)
            dst[start:start + n, :] = src[:, start:start + n].T

    def cast_rows(dst, base):
        def cast(i):
            r = pl.multiple_of(i * 288, 16)
            dst[pl.ds(r, 288), T:2 * T] = dp[pl.ds(pl.multiple_of(base + r, 8), 288), :].astype(bf16)

        loop(GR // 288, cast)

    def take_pair(dst, base, source):
        def cast(i):
            r = pl.multiple_of(i * HD, 16)
            dst[pl.ds(base + r, HD), T:2 * T] = recv[pl.ds(source + r, HD), :].astype(bf16)

        loop(W // HD, cast)

    first_half, second_half = pl.ds(0, W), pl.ds(W, W)
    order = {"far": 0, "right": 1, "left": 2, "own": 3}

    ring_f = {"far": (fa + 2) % 4, "right": (fa + 1) % 4, "left": (fa + 3) % 4, "own": fa}
    fr, fl = first((fa + 1) % 4), first((fa + 3) % 4)
    sr, sl = second((sa + 1) % 4), second((sa + 3) % 4)

    def g_slot(buf):
        def slot(which, h):
            return buf.at[pl.ds(order[which] * CH + h * 144, 144), :]

        return slot

    def p_slot(buf):
        far = {"far": (sa + 2) % 4, "right": (sa + 1) % 4, "left": (sa + 3) % 4}

        def slot(which, h):
            base = far[which] * RP
            if h == 0:
                return buf.at[pl.ds(pl.multiple_of(base, 8), 40), :]
            return buf.at[pl.ds(pl.multiple_of(base + 40, 8), 32), :]

        return slot

    ring_1 = Ring(copies, fl, fr, g_slot(gbuf), box1, 144)
    ring_2 = Ring(copies, fl, fr, g_slot(tbuf), box2, 144)
    ring_3 = Ring(copies, fl, fr, g_slot(tbuf), box3, 144)
    ring_1p = Ring(copies, sl, sr, p_slot(own1), pbox1, 40)
    ring_2p = Ring(copies, sl, sr, p_slot(own2), pbox2, 40)
    ring_3p = Ring(copies, sl, sr, p_slot(own3), pbox3, 40)

    def chunk_of(which):
        rows = pl.ds(pl.multiple_of(ring_f[which] * CH, 16), CH)
        base = 0 if which == "own" else order[which] * CH
        return rows, pl.ds(base, CH)

    def first_pair(which):
        rows, to = chunk_of(which)
        dst = own1 if which == "own" else gbuf
        lo, lt = got[rows, :], tokt[rows, :]
        dst[to, 0:512] = dot_t(lo, rhs1[0:512, :])
        shared = rhs1[512:640, :]
        is_out = lax.broadcasted_iota(jnp.int32, (CH, 128), 1) < W - 512
        dst[to, 512:640] = jnp.where(is_out, dot_t(lo, shared), dot_t(lt, shared))
        dst[to, 640:GC] = dot_t(lt, rhs1[640:GC, :])

    def key_chunk(which):
        rows, to = chunk_of(which)
        dst = own2 if which == "own" else tbuf
        dst[to, :] = dot_t(tokt[rows, :], rhs2[...])

    def moment_chunk(which):
        rows, to = chunk_of(which)
        dst = own3 if which == "own" else tbuf
        dst[to, :] = dot_t(tokt[rows, :], kx[...])

    def add_up(dst, box, rows, tile):
        def step(i):
            r = pl.ds(pl.multiple_of(i * tile, 8), tile)
            dst[r, :] = dst[r, :] + (box[1, r, :] + box[2, r, :])

        loop(rows // tile, step)

    in_tok.wait()
    in_k.wait()
    value = jnp.maximum(dot(wslot[0], tok[...]), 0.0).astype(bf16)
    k = kx.at[pl.ds(0, W), pl.ds(0, T)]
    k[...] = value
    send[first_half, :] = value.astype(f32)
    in_q = local(wq_h, wslot.at[0], in_sem.at[4])
    pl.semaphore_wait(barrier, len(peers))
    pair_k = copies.start(send.at[first_half, :], recv.at[first_half, :], partner)
    in_v.wait()
    value = dot(wslot[1], tok[...]).astype(bf16)
    for h in range(HEADS):
        v[HP * h:HP * h + HD, :] = value[HD * h:HD * h + HD, :]
        v[HP * h + HD:HP * h + HP, :] = sum_row(jnp.ones((1, T), f32)).astype(bf16)
    in_o = local(wo_h, wslot.at[1], in_sem.at[5])
    state_part(sta, k, [v])
    state = State(sta, a0, a1, afin)
    state.step0()
    send_tok = send_rows(tok, 0)

    in_q.wait()
    q[...] = jnp.maximum(dot(wslot[0], tok[...]), 0.0).astype(bf16)
    state.step1()
    own_rows(tok, tokt, GR)
    kx[W:WP, :] = jnp.zeros((WP - W, 2 * T), bf16)
    rhs1[2 * W:GC, :] = jnp.zeros((GC - 2 * W, 2 * T), bf16)
    rhs2[W:WP, :] = jnp.zeros((WP - W, 2 * T), bf16)
    pair_k.wait_recv()
    take_pair(kx, 0, 0)
    send_tok.wait_recv()
    cast_rows(tokt, 0)
    moment_chunk("far")
    ring_3.far()
    in_o.wait()
    in_go.wait()
    gm[...] = dot(wslot[1], go[...]).astype(bf16)
    state.step2()
    moment_chunk("right")
    ring_3.near_right()
    moment_chunk("left")
    ring_3.near_left()
    ring_3.combine()
    send_go = send_rows(go, GR)
    flip(wslot.at[1], wot)
    in_v = local(wv_h, wslot.at[1], in_sem.at[2])
    copies.sent(send_tok)
    own_rows(go, got, 0)
    moment_chunk("own")
    state.step3()
    send_go.wait_recv()
    cast_rows(got, GR)
    flip(wslot.at[0], wqn)
    in_k = local(wk_h, wslot.at[0], in_sem.at[1])
    copies.sent(pair_k)
    state.done()

    dv, ngh, ngl = (tok.at[pl.ds(WP * i, WP), :] for i in range(3))

    def attend(h):
        high, low = parts(afin[head(h), :])
        qt = q[head(h), :]
        both = dot_n(high, qt) + dot_n(low, qt)
        rec = 1.0 / (both[HD:HD + 1, :] + EPS)
        att = both[0:HD, :] * rec
        rhs1[head(h), 0:T] = att.astype(bf16)
        send[head(h), :] = att.astype(bf16).astype(f32)
        g = gm[head(h), :].astype(f32)
        grad = -jnp.sum(g * att, axis=0, keepdims=True) * rec
        high, low = parts(g * rec)
        at = pl.ds(h * HP, HD)
        ngh[at, :] = high
        ngl[at, :] = low
        high, low = parts(sum_row(grad))
        at = pl.ds(h * HP + HD, HP - HD)
        ngh[at, :] = high
        ngl[at, :] = low

    each(HEADS, attend)
    pair_m = copies.start(send.at[first_half, :], recv.at[first_half, :], partner)

    ring_y = {"far": (y + 2) % 4, "right": (y + 1) % 4, "left": (y + 3) % 4, "own": y}
    copies.sent(send_go)

    def y_rows(which):
        return pl.ds(pl.multiple_of(ring_y[which] * W, 16), W)

    def out_chunk(which):
        cp[pl.ds(order[which] * W, W), :] = dot(wot[y_rows(which), :], rhs1[0:W, 0:T])

    def y_slot(buf):
        def slot(which, h):
            return buf.at[pl.ds(order[which] * W + h * (W // 2), W // 2), :]

        return slot

    up, down = along_y((y + 1) % 4), along_y((y + 3) % 4)
    ring_c = Ring(copies, down, up, y_slot(cp), cbox, W // 2)
    out_chunk("far")
    ring_c.far()

    state_part(stb, q, [ngh, ngl])
    state = State(stb, b0, b1, bfin)
    state.step0()

    def query_grad(h):
        high, low = parts(afin[head(h), :])
        ng = ngh[block(h), :]
        value = dot(high, ng) + dot(low, ng) + dot(high, ngl[block(h), :])
        value = jnp.where(q[head(h), :].astype(f32) > 0, value, 0.0).astype(bf16)
        at = pl.ds(W + h * HD, HD)
        rhs1[at, 0:T] = value
        send[at, :] = value.astype(f32)

    each(HEADS, query_grad)
    pair_q = copies.start(send.at[second_half, :], recv.at[second_half, :], partner)
    state.step1()
    ring_3.arrived()
    add_up(own3, box3, CH, 96)
    ring_3p.far()
    ring_3p.near_right()
    ring_3p.near_left()
    pair_m.wait_recv()
    take_pair(rhs1, 0, 0)
    pair_q.wait_recv()
    take_pair(rhs1, W, W)
    first_pair("far")
    ring_1.far()
    out_chunk("right")
    ring_c.near_right()
    out_chunk("left")
    ring_c.near_left()
    first_pair("right")
    first_pair("left")
    state.step2()
    ring_1.near_right()
    ring_1.near_left()
    copies.sent(pair_m)
    copies.sent(pair_q)
    ring_3p.combine()
    in_v.wait()
    flip(wslot.at[1], wvn)
    in_k.wait()
    flip(wslot.at[0], wkn)
    ring_c.combine()
    ring_1.combine()
    first_pair("own")
    state.step3()

    state.done()

    def key_value_grad(h):
        high, low = parts(bfin[head(h), :])
        kt, vt = k[head(h), :], v[block(h), :]
        one = dot(high, vt) + dot(low, vt)
        one = jnp.where(kt.astype(f32) > 0, one, 0.0).astype(bf16)
        rhs2[head(h), 0:T] = one
        send[head(h), :] = one.astype(f32)
        dv[head(h), :] = (dot_n(high, kt) + dot_n(low, kt))[0:HD, :].astype(bf16)

    each(HEADS, key_value_grad)
    pair = copies.start(send.at[first_half, :], recv.at[first_half, :], partner)

    def in_chunk(which):
        rows = y_rows(which)
        dp[pl.ds(order[which] * W, W), :] = (
            dot(wqn[rows, :], rhs1[W:2 * W, 0:T]) + dot(wkn[rows, :], rhs2[0:W, 0:T])
            + dot(wvn[rows, :], dv[0:W, :]))

    ring_d = Ring(copies, down, up, y_slot(dp), dbox, W // 2)
    in_chunk("far")
    ring_d.far()
    pair.wait_recv()
    take_pair(rhs2, 0, 0)
    ring_3.sent(("a0", "a1", "d0", "d1", "c0", "c1"))
    key_chunk("far")
    ring_2.far()
    in_chunk("right")
    ring_d.near_right()
    in_chunk("left")
    ring_d.near_left()
    key_chunk("right")
    ring_2.near_right()
    key_chunk("left")
    ring_2.near_left()
    key_chunk("own")
    out_chunk("own")
    in_chunk("own")

    def final(src, box, out, sem):
        rows = pl.ds(pl.multiple_of(sa * RP, 8), RP)
        src[rows, :] = src[rows, :] + (box[1] + box[2])
        return local(src.at[rows, :], out, sem)

    ring_3p.arrived()
    rows = pl.ds(pl.multiple_of(sa * RP, 8), RP)
    moment = own3[rows, :] + (pbox3[1] + pbox3[2])
    for h in range(HEADS):
        high, low = parts(moment[:, HD * h:HD * h + HD])
        state_high, state_low = parts(bfin[head(h), 0:HD])
        pbox3[0, :, HD * h:HD * h + HD] = (
            dot(high, state_high) + dot(high, state_low) + dot(low, state_high))
    out_3 = local(pbox3.at[0], g3_o, out_sem.at[4])

    ring_1.arrived()
    add_up(own1, box1, CH, 96)
    ring_1p.far()
    ring_1p.near_right()
    ring_1p.near_left()

    def y_sum(buf, box, dst, out, sem):
        def step(i):
            at = pl.ds(pl.multiple_of(3 * W + i * HD, 16), HD)
            rb = pl.ds(pl.multiple_of(i * HD, 16), HD)
            dst[rb, :] = (buf[at, :] + (box[1, rb, :] + box[2, rb, :])).astype(bf16)

        loop(HEADS, step)
        return local(dst, out, sem)

    ring_c.arrived()
    out_c = y_sum(cp, cbox, q, at_o, out_sem.at[0])

    ring_2.combine()
    ring_d.combine()
    ring_1p.combine()
    ring_2.arrived()
    add_up(own2, box2, CH, 96)
    ring_2p.far()
    ring_2p.near_right()
    ring_2p.near_left()
    ring_1p.arrived()
    out_1 = final(own1, pbox1, g1_o, out_sem.at[1])
    ring_2p.combine()
    ring_2p.arrived()
    out_2 = final(own2, pbox2, g2_o, out_sem.at[2])

    ring_d.arrived()
    out_d = y_sum(dp, dbox, gm, gt_o, out_sem.at[3])
    copies.finish()
    for copy in (out_c, out_1, out_2, out_3, out_d):
        copy.wait()


def finish(factor, at, gt, g1, g2, g3, at_o, gt_o, gq_o, gk_o, gv_o, gw_o):
    at_o[...] = at[...]
    gt_o[...] = gt[...]
    one = g1[0:ROWS, :] * factor
    gw_o[...] = one[:, 0:W]
    gq_o[...] = one[:, W:2 * W]
    gk_o[...] = g2[0:ROWS, 0:W] * factor
    gv_o[...] = g3[0:ROWS, 0:W] * factor


def body(tokens, w_query, w_key, w_value, w_out, grad_out):
    shapes = [
        ((D, T), bf16), ((D, T), bf16), ((2, W, D), bf16),
        ((D, W), bf16), ((D, W), bf16), ((D, W), bf16), ((D, W), bf16),
        ((GR, 2 * T), bf16), ((GR, 2 * T), bf16),
        ((W, T), bf16), ((HEADS * HP, T), bf16), ((W, T), bf16), ((WP, 2 * T), bf16),
        ((GC, 2 * T), bf16), ((WP, 2 * T), bf16), ((2 * W, T), f32), ((2 * W, T), f32),
        ((3 * CH, GC), f32), ((3 * CH, WP), f32), ((CH, GC), f32), ((CH, WP), f32), ((CH, WP), f32),
        ((3, CH, GC), f32), ((3, CH, WP), f32), ((3, CH, WP), f32),
        ((3, RP, GC), f32), ((3, RP, WP), f32), ((3, RP, WP), f32),
        ((2 * GR, T), f32), ((2 * GR, T), f32), ((3, W, T), f32), ((3, W, T), f32),
    ]
    for _ in range(2):
        shapes += [((SR, HP), f32), ((SR // 2, HP), f32), ((NB - 1, PR, HP), f32), ((SR, HP), f32)]
    scratch = [pltpu.VMEM(*shape) for shape in shapes]
    scratch += [
        pltpu.SemaphoreType.DMA((6,)), pltpu.SemaphoreType.DMA((5,)),
        pltpu.SemaphoreType.DMA((120,)), pltpu.SemaphoreType.DMA((120,)),
    ]
    spaces = [pl.BlockSpec(memory_space=pl.ANY)] * 6
    at, gt, g1, g2, g3 = pl.pallas_call(
        kernel,
        out_shape=(
            jax.ShapeDtypeStruct((W, T), bf16), jax.ShapeDtypeStruct((W, T), bf16),
            jax.ShapeDtypeStruct((RP, GC), f32), jax.ShapeDtypeStruct((RP, WP), f32),
            jax.ShapeDtypeStruct((RP, WP), f32),
        ),
        in_specs=spaces,
        out_specs=spaces[:5],
        scratch_shapes=scratch,
        compiler_params=pltpu.CompilerParams(
            collective_id=0, has_side_effects=True, vmem_limit_bytes=64 * 1024 * 1024 - 65536),
        cost_estimate=pl.CostEstimate(flops=16 * 10**9, bytes_accessed=16 * 10**6, transcendentals=0),
        name="fused_attention",
    )(tokens.T, w_query.T, w_key.T, w_value.T, w_out, grad_out.T)
    factor = 1.0 / math.sqrt(T * lax.axis_size("seq"))
    grad = jax.ShapeDtypeStruct((ROWS, W), f32)
    vmem = pl.BlockSpec(memory_space=pltpu.VMEM)
    at, gt, gq, gk, gv, gw = pl.pallas_call(
        functools.partial(finish, factor),
        out_shape=(
            jax.ShapeDtypeStruct((W, T), bf16), jax.ShapeDtypeStruct((W, T), bf16),
            grad, grad, grad, grad,
        ),
        in_specs=[vmem] * 5,
        out_specs=[vmem] * 6,
        name="final_arrays",
    )(at, gt, g1, g2, g3)
    return (at.T, gt.T, gq, gk, gv, gw.T)


def solution(mesh):
    in_specs = (
        P("seq", None),
        P(None, "head"),
        P(None, "head"),
        P(None, "head"),
        P("head", None),
        P("seq", None),
    )
    out_specs = (
        P("seq", "head"),
        P("seq", "head"),
        P("seq", "head"),
        P("seq", "head"),
        P("seq", "head"),
        P("head", "seq"),
    )
    return jax.shard_map(body, mesh=mesh, in_specs=in_specs, out_specs=out_specs, check_vma=False)
```
